32 devices in a mesh: parts: 2 (over y), rows: 8 (over z, x), head: 2 (over core).
Axes of the slice: x: 2, y: 2, z: 4, core: 2. Of those that a mesh axis runs over, the one named last changes fastest.
Arguments:
- prefill_states: bfloat16 [16, 128, 32, 128], P(('parts', 'rows'), 'head'), parts along dimension 0, may hold values from -0.5 to 0.5
- src_slot: int32 [16], P('parts'), parts along dimension 0, may hold values from 0 to 7, each once
- dst_slot: int32 [16], P('parts'), parts along dimension 0, may hold values from 0 to 15, as said below
- resident_states: bfloat16 [32, 128, 32, 128], P(('parts', 'rows'), 'head'), parts along dimension 0, may hold values from -0.5 to 0.5
- x_new: bfloat16 [4, 32, 128, 32], P(None, ('parts', 'rows'), 'head'), parts along dimension 1, may hold values from -6 to 6
- z_gate: bfloat16 [4, 32, 128, 32], P(None, ('parts', 'rows'), 'head'), parts along dimension 1, may hold values from -6 to 6
- dt_raw: float32 [4, 32, 128], P(None, ('parts', 'rows'), 'head'), parts along dimension 1, may hold values from -5 to 5
- b_in: bfloat16 [4, 32, 4, 128], P(None, ('parts', 'rows')), parts along dimension 1, may hold values from -0.59765625 to 0.59765625
- c_in: bfloat16 [4, 32, 4, 128], P(None, ('parts', 'rows')), parts along dimension 1, may hold values from -6 to 6
- a_rate: float32 [128], P('head'), may hold values from 0.05 to 3
- dt_bias: float32 [128], P('head'), may hold values from -1.5 to 0.5
- skip_d: float32 [128], P('head'), may hold values from 0.5 to 1.5
- norm_gain: float32 [128, 32], P('head'), may hold values from 0.1 to 1.9
Outputs:
- decoded: bfloat16 [4, 32, 128, 32], P(None, ('parts', 'rows'), 'head'), parts along dimension 1
- final_states: bfloat16 [32, 128, 32, 128], P(('parts', 'rows'), 'head'), parts along dimension 0
The draws below stay inside these ranges and needn't reach their ends.
There are 2 independent parts, one for each index of `parts`. The reference program is written for one: setup_inputs(seed, part) draws one part's arguments, and reference() takes and returns one part's arrays. A program takes and returns all parts, laid end to end along the dimension named above; an argument that names none is the same for every part. Nothing has to cross between parts.
Inputs may be any that keep to these rules, and one draw needn't show every extreme that they name: `dst_slot`: distinct decode rows; the 2 rows of some one index of rows are all listed. `src_slot`: each prefill slot is named once.
All inputs are finite; a program needn't handle non-finite values.
Results may differ from the reference program's by a relative error of at most 0.001.
Values may be sent and summed in bfloat16 or wider, within the bound.
No kernel may reach another device: no remote copies, remote signals or barrier semaphores. Data moves between devices by JAX's collectives and lax.ppermute only.
A program may use at most 64 MiB of HBM per device.

```python
import math
import jax
import jax.numpy as jnp
from jax import lax

HEADS = 128
HEAD_DIM = 32
STATE = 128
GROUPS = 4
STEPS = 4
ROW_DEV = 2
ROWS = 16
LIST = 8


def draw_dst_slot(key, part):
    key = jax.random.fold_in(key, 11)
    key_order, key_busy, key_mix = jax.random.split(key, 3)
    ranking = jax.random.permutation(key_order, ROWS).astype(jnp.int32)
    busiest = jax.random.randint(key_busy, (), 0, ROWS // ROW_DEV).astype(jnp.int32)
    position = jnp.arange(ROWS, dtype=jnp.int32)
    scores = jnp.where(position // ROW_DEV == busiest, position % ROW_DEV - ROW_DEV, ranking)
    scores = jnp.where(position == 0, -ROW_DEV - 1, scores)
    scores = jnp.where(position == ROWS - 1, -ROW_DEV - 2, scores)
    chosen = jnp.argsort(scores, stable=True)[:LIST].astype(jnp.int32)
    return jax.random.permutation(key_mix, chosen).astype(jnp.int32)


def shard_levels(key, extent, cuts, smallest, top_value):
    loudness, own = 1.0, jax.random.fold_in(key, 6)
    for dim, blocks in cuts:
        steps = jnp.exp(jax.random.uniform(jax.random.fold_in(own, dim), (blocks,), jnp.float32, smallest / len(cuts), top_value / len(cuts)))
        loudness = loudness * jnp.repeat(steps, extent[dim] // blocks).reshape([-1 if axis == dim else 1 for axis in range(len(extent))])
    return loudness


def bell_draw(stream_key, dims, spread, reach, pieces=(), kind=jnp.bfloat16):
    entries = spread * jax.random.normal(stream_key, dims, jnp.float32)
    if pieces:
        entries = entries * shard_levels(stream_key, dims, pieces, -0.22, 0.18)
    return jnp.clip(entries, -reach, reach).astype(kind)


def setup_inputs(seed: int = 0, part: int = 0) -> dict:
    streams_of = jax.random.split(jax.random.key(seed), 14)
    part_splits = jax.random.split(jax.random.fold_in(streams_of[13], part), 14)
    return {
        "prefill_states": bell_draw(part_splits[0], (LIST, HEADS, HEAD_DIM, STATE), STATE ** -0.5, 0.5, ((0, 8), (1, 2))),
        "src_slot": jax.random.permutation(part_splits[1], LIST).astype(jnp.int32),
        "dst_slot": draw_dst_slot(jax.random.fold_in(jax.random.fold_in(streams_of[13], part), 71), part),
        "resident_states": bell_draw(part_splits[3], (ROWS, HEADS, HEAD_DIM, STATE), STATE ** -0.5, 0.5, ((0, 8), (1, 2))),
        "x_new": bell_draw(part_splits[4], (STEPS, ROWS, HEADS, HEAD_DIM), 1.0, 6.0, ((1, 8), (2, 2))),
        "z_gate": bell_draw(part_splits[5], (STEPS, ROWS, HEADS, HEAD_DIM), 1.0, 6.0, ((1, 8), (2, 2))),
        "dt_raw": bell_draw(part_splits[6], (STEPS, ROWS, HEADS), 1.0, 5.0, ((1, 8), (2, 2)), jnp.float32),
        "b_in": bell_draw(part_splits[7], (STEPS, ROWS, GROUPS, STATE), 0.1, 0.59765625, ((1, 8),)),
        "c_in": bell_draw(part_splits[8], (STEPS, ROWS, GROUPS, STATE), 1.0, 6.0, ((1, 8),)),
        "a_rate": jnp.clip(jnp.exp(math.log(3.0) - 4.0943445 * jax.random.uniform(streams_of[9], (HEADS,), jnp.float32) ** shard_levels(streams_of[9], (HEADS,), ((0, 2),), -0.2, 0.2)), 0.05, 3.0),
        "dt_bias": jnp.clip(-1.5 + 2.0 * jax.random.uniform(streams_of[10], (HEADS,), jnp.float32) ** shard_levels(streams_of[10], (HEADS,), ((0, 2),), -0.2, 0.2), -1.5, 0.5),
        "skip_d": jnp.clip(0.5 + 1.0 * jax.random.uniform(streams_of[11], (HEADS,), jnp.float32) ** shard_levels(streams_of[11], (HEADS,), ((0, 2),), -0.2, 0.2), 0.5, 1.5),
        "norm_gain": jnp.clip(1.0 + 0.18 * jax.random.normal(streams_of[12], (HEADS, HEAD_DIM), jnp.float32), 0.1, 1.9),
    }


def advance(hidden_state, x_steps, z_steps, dt_steps, b_steps, c_steps, rate, bias, skip_gain, gain):
    outputs = []
    for step_index in range(x_steps.shape[0]):
        inputs = x_steps[step_index].astype(jnp.float32)
        step_size = jax.nn.softplus(dt_steps[step_index] + bias[None, :])
        retained = jnp.exp(-rate[None, :] * step_size)
        b_now = b_steps[step_index].astype(jnp.float32)
        c_now = c_steps[step_index].astype(jnp.float32)
        hidden_state = retained[:, :, None, None] * hidden_state + (step_size[:, :, None] * inputs)[:, :, :, None] * b_now[:, :, None, :]
        readout = lax.optimization_barrier(jnp.sum(hidden_state * c_now[:, :, None, :], axis=-1)) + skip_gain[None, :, None] * inputs
        gated_out = readout * jax.nn.silu(z_steps[step_index].astype(jnp.float32))
        squares = lax.optimization_barrier(jnp.mean(gated_out * gated_out, axis=(1, 2), keepdims=True))
        normed = gated_out * lax.rsqrt(squares + 1e-05) * gain[None]
        outputs.append(normed.astype(jnp.bfloat16))
    return (jnp.stack(outputs), hidden_state.astype(jnp.bfloat16))

def reference(prefill_states, src_slot, dst_slot, resident_states, x_new, z_gate, dt_raw, b_in, c_in, a_rate, dt_bias, skip_d, norm_gain):
    per_group = HEADS // GROUPS
    matches = jnp.arange(ROWS, dtype=jnp.int32)[:, None] == dst_slot[None, :]
    listed = jnp.any(matches, axis=1)
    source = lax.optimization_barrier(jnp.sum(jnp.where(matches, src_slot[None, :], 0), axis=1)).astype(jnp.int32)

    def one_group(group_id):
        head_start = (group_id * per_group).astype(jnp.int32)
        incoming = jnp.take(lax.dynamic_slice_in_dim(prefill_states, head_start, per_group, 1), source, axis=0)
        staying = lax.dynamic_slice_in_dim(resident_states, head_start, per_group, 1)
        initial = jnp.where(listed[:, None, None, None], incoming, staying).astype(jnp.float32)
        return advance(initial, lax.dynamic_slice_in_dim(x_new, head_start, per_group, 2), lax.dynamic_slice_in_dim(z_gate, head_start, per_group, 2), lax.dynamic_slice_in_dim(dt_raw, head_start, per_group, 2), lax.dynamic_slice_in_dim(b_in, group_id, 1, 2), lax.dynamic_slice_in_dim(c_in, group_id, 1, 2), lax.dynamic_slice_in_dim(a_rate, head_start, per_group, 0), lax.dynamic_slice_in_dim(dt_bias, head_start, per_group, 0), lax.dynamic_slice_in_dim(skip_d, head_start, per_group, 0), lax.dynamic_slice_in_dim(norm_gain, head_start, per_group, 0))
    decoded, finals = lax.map(one_group, jnp.arange(GROUPS, dtype=jnp.int32))
    decoded = jnp.moveaxis(decoded, 0, 2).reshape(STEPS, ROWS, HEADS, HEAD_DIM)
    finals = jnp.moveaxis(finals, 0, 1).reshape(ROWS, HEADS, HEAD_DIM, STATE)
    return (decoded, finals)
```

```python
import functools

import jax
import jax.numpy as jnp
from jax import lax
from jax.experimental import pallas as pl
from jax.experimental.pallas import tpu as pltpu
from jax.sharding import PartitionSpec as P

HEADS = 128
GROUPS = 4
F32 = jnp.float32
BF16 = jnp.bfloat16


def split_terms(value):
    terms = []
    for _ in range(3):
        head = lax.reduce_precision(value, 8, 7)
        terms.append(head)
        value = value - head
    return terms


def gather_kernel(count, slots_ref, held_ref, out_ref, sem):
    def copy(i):
        return pltpu.make_async_copy(held_ref.at[slots_ref[i]], out_ref.at[i], sem.at[i])

    for i in range(count):
        copy(i).start()
    for i in range(count):
        copy(i).wait()


def gather_pieces(slots, held):
    count = slots.shape[0]
    return pl.pallas_call(
        functools.partial(gather_kernel, count),
        grid_spec=pltpu.PrefetchScalarGridSpec(
            num_scalar_prefetch=1,
            grid=(1,),
            in_specs=[pl.BlockSpec(memory_space=pl.ANY)],
            out_specs=pl.BlockSpec(memory_space=pl.ANY),
            scratch_shapes=[pltpu.SemaphoreType.DMA((count,))],
        ),
        out_shape=jax.ShapeDtypeStruct((count,) + held.shape[1:], held.dtype),
    )(slots, held)


def decode_kernel(
    rows, groups, pieces, info_ref, recv_ref, resident_ref, c_ref, left_ref, right_ref,
    carry_ref, base_ref, gate_ref, gain_ref, decoded_ref, final_ref, state, sem,
):
    span = recv_ref.shape[2]

    def each(r, act):
        listed = info_ref[r]
        mask = info_ref[rows + r]

        def piece(q):
            here = pl.ds(pl.multiple_of(q * span, 16), span)

            @pl.when(listed == 1)
            def _():
                act(pltpu.make_async_copy(
                    recv_ref.at[q ^ mask, r], state.at[r, here], sem.at[r]))

            @pl.when(listed == 0)
            def _():
                act(pltpu.make_async_copy(
                    resident_ref.at[r, here], state.at[r, here], sem.at[r]))

        if pieces <= 8:
            for q in range(pieces):
                piece(q)
        else:
            pl.loop(0, pieces)(piece)

    for r in range(rows):
        each(r, lambda copy: copy.start())
    for r in range(rows):
        each(r, lambda copy: copy.wait())
    block = state.shape[1] // groups
    for g in range(groups):
        lanes = slice(g * block, (g + 1) * block)
        seen = None
        for r in range(rows):
            initial = state[r, lanes]
            part = lax.dot_general(
                c_ref[r, g], initial, (((1,), (1,)), ((), ())), preferred_element_type=F32)
            seen = part if seen is None else seen + part
            moved = lax.dot_general(
                left_ref[r, :, lanes], right_ref[r, g], (((0,), (0,)), ((), ())),
                preferred_element_type=F32)
            width = initial.shape[1]
            final_ref[r, lanes] = (
                moved[:, width:] * initial.astype(F32) + moved[:, :width]).astype(BF16)
        readout = carry_ref[:, lanes] * seen + base_ref[:, lanes]
        gated = readout * gate_ref[:, lanes]
        squares = jnp.mean(gated * gated, axis=1, keepdims=True)
        normed = gated * lax.rsqrt(squares + 1e-05) * gain_ref[:, lanes]
        decoded_ref[:, lanes] = normed.astype(BF16)


def decode(info, recv, resident, c_rows, left, right, carry, base, gate, gain):
    rows, flat, entries = resident.shape
    groups = c_rows.shape[1]
    whole = pl.BlockSpec(memory_space=pltpu.VMEM)
    anywhere = pl.BlockSpec(memory_space=pl.ANY)
    return pl.pallas_call(
        functools.partial(decode_kernel, rows, groups, recv.shape[0]),
        grid_spec=pltpu.PrefetchScalarGridSpec(
            num_scalar_prefetch=1,
            grid=(1,),
            in_specs=[anywhere, anywhere] + [whole] * 7,
            out_specs=[whole, whole],
            scratch_shapes=[
                pltpu.VMEM((rows, flat, entries), BF16),
                pltpu.SemaphoreType.DMA((rows,)),
            ],
        ),
        out_shape=[
            jax.ShapeDtypeStruct(base.shape, BF16),
            jax.ShapeDtypeStruct((rows, flat, entries), BF16),
        ],
        compiler_params=pltpu.CompilerParams(vmem_limit_bytes=32 * 1024 * 1024),
    )(info, recv, resident, c_rows, left, right, carry, base, gate, gain)


def prepare(x_new, z_gate, dt_raw, b_in, c_in, a_rate, dt_bias, skip_d, norm_gain):
    steps, rows, heads, channels = x_new.shape
    groups, entries = b_in.shape[2:]
    flat = heads * channels

    def over_channels(value):
        return jnp.broadcast_to(value[..., None], value.shape + (channels,)).reshape(
            value.shape[:-1] + (flat,))

    x = x_new.reshape(steps, rows, flat).astype(F32)
    delta = jax.nn.softplus(dt_raw + dt_bias)
    kept = jnp.exp(-a_rate * delta)
    bc = jnp.sum(
        c_in.astype(F32)[:, None] * b_in.astype(F32)[None], axis=-1)
    bc = jnp.repeat(bc, heads // groups, axis=-1)
    carry, weights, factors = [], [], []
    for t in range(steps):
        carry.append(kept[t] if t == 0 else carry[-1] * kept[t])
        weights = [w * kept[t] for w in weights] + [delta[t]]
        for s in range(t + 1):
            factor = weights[s] * bc[t, s]
            factors.append(factor + skip_d if s == t else factor)
    lanes = over_channels(jnp.stack(factors + carry + weights))
    base, at = [], 0
    for t in range(steps):
        base.append(sum(lanes[at + s] * x[s] for s in range(t + 1)))
        at += t + 1
    carry_lanes = lanes[at:at + steps]
    moved = lanes[at + steps:] * x
    left = [p[s] for p in split_terms(moved) for s in range(steps)]
    left += split_terms(carry_lanes[-1])
    left.append(jnp.zeros_like(left[0]))
    left = jnp.stack(left, axis=1).astype(BF16)
    b_rows = jnp.moveaxis(b_in, 0, 2)
    none = jnp.zeros((rows, groups, 3 * steps, entries), BF16)
    ones = jnp.ones((rows, groups, 3, entries), BF16)
    right = jnp.concatenate([
        jnp.concatenate([b_rows] * 3 + [none[:, :, :4]], 2),
        jnp.concatenate([none, ones, none[:, :, :1]], 2),
    ], 3)
    own = jnp.eye(rows, dtype=BF16)[:, None, None, :, None]
    c_rows = jnp.moveaxis(c_in, 0, 2)[:, :, :, None] * own
    gate = jax.nn.silu(z_gate.reshape(steps, rows, flat).astype(F32))
    both = steps * rows
    return (
        c_rows.reshape(rows, groups, both, entries),
        left,
        right,
        carry_lanes.reshape(both, flat),
        jnp.stack(base).reshape(both, flat),
        gate.reshape(both, flat),
        norm_gain.reshape(1, flat),
    )


def local(
    prefill_states, src_slot, dst_slot, resident_states, x_new, z_gate, dt_raw, b_in, c_in,
    a_rate, dt_bias, skip_d, norm_gain,
):
    row_count, local_heads, channels, entries = resident_states.shape
    flat = local_heads * channels
    shards = lax.axis_size("rows")
    me = lax.axis_index("rows")
    quarter = shards // 2
    matches = jnp.arange(shards * row_count, dtype=jnp.int32)[:, None] == dst_slot[None, :]
    listed = jnp.any(matches, axis=1).astype(jnp.int32)
    source = jnp.sum(jnp.where(matches, src_slot[None, :], 0), axis=1)

    span = flat // quarter
    pieces = prefill_states.reshape(quarter, span, entries)
    few = shards == 8
    if few:
        held = [pieces[0]]
        for k in range(1, shards):
            held.append(lax.ppermute(
                pieces[k % quarter], "rows", [(i, i ^ k) for i in range(shards)]))
        held = jnp.stack(held)
        slots = source ^ me
        mask = source % quarter
    else:
        held = lax.all_to_all(
            jnp.concatenate([pieces, pieces]), "rows", split_axis=0, concat_axis=0, tiled=True)
        slots = source
        mask = jnp.zeros_like(source)
    half_rows = quarter * row_count
    slots = lax.dynamic_slice_in_dim(slots, (me // quarter) * half_rows, half_rows)
    halves = [[h * quarter + i for i in range(quarter)] for h in range(2)]
    sent = gather_pieces(slots, held).reshape(quarter, row_count * span, entries)
    recv = lax.all_to_all(
        sent, "rows", split_axis=0, concat_axis=0, tiled=True, axis_index_groups=halves)
    recv = recv.reshape(quarter, row_count, span, entries)

    groups = local_heads // (HEADS // GROUPS)
    group_base = lax.axis_index("head") * groups
    ready = prepare(
        x_new, z_gate, dt_raw,
        lax.dynamic_slice_in_dim(b_in, group_base, groups, 2),
        lax.dynamic_slice_in_dim(c_in, group_base, groups, 2),
        a_rate, dt_bias, skip_d, norm_gain)
    info = jnp.concatenate([
        lax.dynamic_slice_in_dim(listed, me * row_count, row_count),
        lax.dynamic_slice_in_dim(mask, me * row_count, row_count)])
    decoded, final = decode(
        info, recv, resident_states.reshape(row_count, flat, entries), *ready)
    return (decoded.reshape(x_new.shape), final.reshape(resident_states.shape))


def solution(mesh):
    placed = (
        P(("parts", "rows"), "head", None, None),
        P("parts"),
        P("parts"),
        P(("parts", "rows"), "head", None, None),
        P(None, ("parts", "rows"), "head", None),
        P(None, ("parts", "rows"), "head", None),
        P(None, ("parts", "rows"), "head"),
        P(None, ("parts", "rows"), None, None),
        P(None, ("parts", "rows"), None, None),
        P("head"),
        P("head"),
        P("head"),
        P("head", None),
    )
    return jax.shard_map(
        local,
        mesh=mesh,
        in_specs=placed,
        out_specs=(
            P(None, ("parts", "rows"), "head", None),
            P(("parts", "rows"), "head", None, None),
        ),
        check_vma=False,
    )
```

```python
import functools

import jax
import jax.numpy as jnp
from jax import lax
from jax.experimental import pallas as pl
from jax.experimental.pallas import tpu as pltpu
from jax.sharding import PartitionSpec as P

HEADS = 128
GROUPS = 4
F32 = jnp.float32
BF16 = jnp.bfloat16
VMEM = pl.BlockSpec(memory_space=pltpu.VMEM)
SMEM = pl.BlockSpec(memory_space=pltpu.SMEM)
ANY = pl.BlockSpec(memory_space=pl.ANY)


def gather_kernel(group, slots_ref, held_ref, out_ref):
    count = out_ref.shape[0]

    def one(i):
        out_ref[i] = held_ref[slots_ref[i], group]

    if count <= 16:
        for i in range(count):
            one(i)
    else:
        pl.loop(0, count)(one)


def gather_pieces(group, slots, held):
    return pl.pallas_call(
        functools.partial(gather_kernel, group),
        in_specs=[SMEM, VMEM],
        out_specs=VMEM,
        out_shape=jax.ShapeDtypeStruct(slots.shape + held.shape[2:], held.dtype),
        compiler_params=pltpu.CompilerParams(vmem_limit_bytes=4 * 1024 * 1024),
    )(slots, held)


def split_terms(value):
    terms = []
    for _ in range(3):
        head = value.astype(BF16).astype(F32)
        terms.append(head)
        value = value - head
    return terms


def prepare_kernel(
    rows, x_ref, z_ref, dt_ref, b_ref, c_ref, head_ref,
    base_ref, carry_ref, gate_ref, left_ref, right_ref, seen_ref,
):
    both, flat = x_ref.shape
    steps = both // rows
    groups = b_ref.shape[0]
    entries = b_ref.shape[2]
    width = flat // groups
    row = lax.broadcasted_iota(jnp.int32, (both, 1), 0)

    def earlier(value, by):
        return value if by == 0 else pltpu.roll(value, by * rows, 0)

    x = x_ref[...].astype(F32)
    z = z_ref[...].astype(F32)
    gate_ref[...] = z / (1.0 + jnp.exp(-z))
    rate, bias, skip = head_ref[0:1], head_ref[1:2], head_ref[2:3]
    logit = dt_ref[...] + bias
    delta = jnp.maximum(logit, 0.0) + jnp.log1p(jnp.exp(-jnp.abs(logit)))
    kept = jnp.exp(-rate * delta)
    carry = kept
    later = jnp.where(row < both - rows, pltpu.roll(kept, both - rows, 0), 1.0)
    reach = 1
    rest = later
    while reach < steps:
        carry = carry * jnp.where(row >= reach * rows, earlier(carry, reach), 1.0)
        rest = rest * jnp.where(
            row < both - reach * rows, pltpu.roll(rest, both - reach * rows, 0), 1.0)
        reach *= 2
    carry_ref[...] = carry

    base = skip * x
    weight = jnp.ones_like(kept)
    for by in range(steps):
        if by:
            weight = weight * earlier(kept, by - 1)
        term = weight * earlier(delta, by) * earlier(x, by)
        parts = []
        for g in range(groups):
            b = b_ref[g].astype(F32)
            c = c_ref[g].astype(F32)
            match = jnp.sum(c * earlier(b, by), axis=1, keepdims=True)
            parts.append(match * term[:, g * width:(g + 1) * width])
        total = jnp.concatenate(parts, axis=1)
        base = base + jnp.where(row >= by * rows, total, 0.0)
    base_ref[...] = base

    left = split_terms(delta * rest * x) + split_terms(carry)
    left_ref[...] = jnp.concatenate(left, axis=0).astype(BF16)
    none = jnp.zeros((3 * both, entries), F32)
    for g in range(groups):
        b = b_ref[g].astype(F32)
        c = c_ref[g].astype(F32)
        right, seen = [], []
        for r in range(rows):
            mine = row % rows == r
            last = jnp.where(row == both - rows + r, 1.0, 0.0) + jnp.zeros((both, entries), F32)
            picked = jnp.where(mine, b, 0.0)
            right.append(jnp.concatenate([picked] * 3 + [none], axis=0))
            right.append(jnp.concatenate([none] + [last] * 3, axis=0))
            seen.append(jnp.where(mine, c, 0.0))
        right_ref[g] = jnp.concatenate(right, axis=1).astype(BF16)
        seen_ref[g] = jnp.concatenate(seen, axis=1).astype(BF16)


def prepare(x_new, z_gate, dt_raw, b_in, c_in, a_rate, dt_bias, skip_d):
    steps, rows, heads, channels = x_new.shape
    groups, entries = b_in.shape[2:]
    flat = heads * channels
    both = steps * rows

    def over_channels(value):
        return jnp.broadcast_to(value[..., None], value.shape + (channels,)).reshape(
            value.shape[0], flat)

    def wide(*shape):
        return jax.ShapeDtypeStruct(shape, F32 if len(shape) == 2 else BF16)

    return pl.pallas_call(
        functools.partial(prepare_kernel, rows),
        in_specs=[VMEM] * 6,
        out_specs=[VMEM] * 6,
        out_shape=[
            wide(both, flat), wide(both, flat), wide(both, flat),
            jax.ShapeDtypeStruct((6 * both, flat), BF16),
            wide(groups, 6 * both, 2 * rows * entries),
            wide(groups, both, rows * entries),
        ],
        compiler_params=pltpu.CompilerParams(vmem_limit_bytes=8 * 1024 * 1024),
    )(
        x_new.reshape(both, flat), z_gate.reshape(both, flat),
        over_channels(dt_raw.reshape(both, heads)),
        jnp.moveaxis(b_in, 2, 0).reshape(groups, both, entries),
        jnp.moveaxis(c_in, 2, 0).reshape(groups, both, entries),
        over_channels(jnp.stack([a_rate, dt_bias, skip_d])),
    )


def decode_kernel(rows, groups, parts, info_ref, *refs):
    recv_refs, refs = refs[:groups * parts], refs[groups * parts:]
    (resident_ref, base_ref, carry_ref, gate_ref, left_ref, right_ref, seen_ref, gain_ref,
     decoded_ref, final_ref, state, ready, sem, out_sem) = refs
    pieces, span = recv_refs[0].shape[0] * parts, recv_refs[0].shape[2]
    block, entries = state.shape[1] // groups, state.shape[2]

    def each(g, r, act):
        listed = info_ref[r]
        mask = info_ref[rows + r]

        def piece(q):
            here = pl.ds(pl.multiple_of(g * block + q * span, 16), span)
            spot = q ^ mask
            for p in range(parts):
                recv_ref = recv_refs[g * parts + p]

                @pl.when((listed == 1) & ((spot == p) | (parts == 1)))
                def _():
                    act(pltpu.make_async_copy(
                        recv_ref.at[spot if parts == 1 else 0, r], state.at[r, here],
                        sem.at[g, r]))

        @pl.when(listed == 0)
        def _():
            here = pl.ds(g * block, block)
            act(pltpu.make_async_copy(
                resident_ref.at[r, here], state.at[r, here], sem.at[g, r]))

        if pieces <= 8:
            for q in range(pieces):
                piece(q)
        else:
            pl.loop(0, pieces)(piece)

    def result(g, r):
        here = pl.ds(g * block, block)
        return pltpu.make_async_copy(
            ready.at[r, here], final_ref.at[r, here], out_sem.at[g, r])

    for g in range(groups):
        for r in range(rows):
            each(g, r, lambda copy: copy.start())
    for g in range(groups):
        for r in range(rows):
            each(g, r, lambda copy: copy.wait())
        lanes = slice(g * block, (g + 1) * block)
        step = 256
        for first in range(g * block, (g + 1) * block, step):
            here = slice(first, first + step)
            moved = lax.dot_general(
                left_ref[:, here], right_ref[g], (((0,), (0,)), ((), ())),
                preferred_element_type=F32)
            for r in range(rows):
                at = 2 * r * entries
                ready[r, here] = (
                    moved[:, at + entries:at + 2 * entries] * state[r, here].astype(F32)
                    + moved[:, at:at + entries]).astype(BF16)
        for r in range(rows):
            result(g, r).start()
        initial = jnp.concatenate([state[r, lanes] for r in range(rows)], axis=1)
        seen = lax.dot_general(
            seen_ref[g], initial, (((1,), (1,)), ((), ())), preferred_element_type=F32)
        readout = carry_ref[:, lanes] * seen + base_ref[:, lanes]
        gated = readout * gate_ref[:, lanes]
        squares = jnp.mean(gated * gated, axis=1, keepdims=True)
        normed = gated * lax.rsqrt(squares + 1e-05) * gain_ref[:, lanes]
        decoded_ref[:, lanes] = normed.astype(BF16)
    for g in range(groups):
        for r in range(rows):
            result(g, r).wait()


def decode(info, recv, resident, ready, gain):
    rows, flat, entries = resident.shape
    groups, parts = len(recv), len(recv[0])
    return pl.pallas_call(
        functools.partial(decode_kernel, rows, groups, parts),
        in_specs=[SMEM] + [ANY] * (1 + groups * parts) + [VMEM] * 7,
        out_specs=[VMEM, ANY],
        scratch_shapes=[
            pltpu.VMEM((rows, flat, entries), BF16),
            pltpu.VMEM((rows, flat, entries), BF16),
            pltpu.SemaphoreType.DMA((groups, rows)),
            pltpu.SemaphoreType.DMA((groups, rows)),
        ],
        out_shape=[
            jax.ShapeDtypeStruct(ready[0].shape, BF16),
            jax.ShapeDtypeStruct((rows, flat, entries), BF16),
        ],
        compiler_params=pltpu.CompilerParams(vmem_limit_bytes=16 * 1024 * 1024),
    )(info, *[part for group in recv for part in group], resident, *ready, gain)


def local(
    prefill_states, src_slot, dst_slot, resident_states, x_new, z_gate, dt_raw, b_in, c_in,
    a_rate, dt_bias, skip_d, norm_gain,
):
    row_count, local_heads, channels, entries = resident_states.shape
    flat = local_heads * channels
    shards = lax.axis_size("rows")
    me = lax.axis_index("rows")
    quarter = shards // 2
    matches = jnp.arange(shards * row_count, dtype=jnp.int32)[:, None] == dst_slot[None, :]
    listed = jnp.any(matches, axis=1).astype(jnp.int32)
    source = jnp.sum(jnp.where(matches, src_slot[None, :], 0), axis=1)

    groups = local_heads // (HEADS // GROUPS)
    span = flat // quarter // groups
    half_rows = quarter * row_count
    halves = [[h * quarter + i for i in range(quarter)] for h in range(2)]

    def exchange(value, groups=None):
        return lax.all_to_all(
            value, "rows", split_axis=0, concat_axis=0, tiled=True, axis_index_groups=groups)

    def hand(value, k):
        return lax.ppermute(value, "rows", [(i, i ^ k) for i in range(shards)])

    pieces = prefill_states.reshape(groups, quarter, span, entries)
    here = jnp.arange(shards * row_count, dtype=jnp.int32) // row_count
    if shards == 8:
        held = jnp.stack([pieces[:, 0]] + [
            hand(pieces[:, k % quarter], k) for k in range(1, shards)])
        slots = source ^ me
        mask = (source ^ here) % quarter
    else:
        pieces = jnp.moveaxis(pieces, 0, 1)
        held = exchange(jnp.concatenate([pieces, pieces]).reshape(
            shards, groups * span, entries)).reshape(shards, groups, span, entries)
        slots = source
        mask = jnp.zeros_like(source)
    slots = lax.dynamic_slice_in_dim(slots, (me // quarter) * half_rows, half_rows)
    own = lax.dynamic_slice_in_dim(mask, me * row_count, row_count)
    recv = []
    if shards == 8:
        order = (jnp.arange(quarter)[:, None] ^ (me % quarter)) * row_count + jnp.arange(row_count)
        slots = slots[order.reshape(half_rows)]
    for g in range(groups):
        sent = gather_pieces(g, slots, held).reshape(quarter, row_count, span, entries)
        if shards == 8:
            recv.append([sent[:1]] + [hand(sent[k:k + 1], k) for k in range(1, quarter)])
        else:
            sent = exchange(sent.reshape(quarter, row_count * span, entries), halves)
            recv.append([sent.reshape(quarter, row_count, span, entries)])

    groups = local_heads // (HEADS // GROUPS)
    group_base = lax.axis_index("head") * groups
    ready = prepare(
        x_new, z_gate, dt_raw,
        lax.dynamic_slice_in_dim(b_in, group_base, groups, 2),
        lax.dynamic_slice_in_dim(c_in, group_base, groups, 2),
        a_rate, dt_bias, skip_d)
    info = jnp.concatenate([
        lax.dynamic_slice_in_dim(listed, me * row_count, row_count), own])
    decoded, final = decode(
        info, recv, resident_states.reshape(row_count, flat, entries), ready,
        norm_gain.reshape(1, flat))
    return (decoded.reshape(x_new.shape), final.reshape(resident_states.shape))


def solution(mesh):
    placed = (
        P(("parts", "rows"), "head", None, None),
        P("parts"),
        P("parts"),
        P(("parts", "rows"), "head", None, None),
        P(None, ("parts", "rows"), "head", None),
        P(None, ("parts", "rows"), "head", None),
        P(None, ("parts", "rows"), "head"),
        P(None, ("parts", "rows"), None, None),
        P(None, ("parts", "rows"), None, None),
        P("head"),
        P("head"),
        P("head"),
        P("head", None),
    )
    return jax.shard_map(
        local,
        mesh=mesh,
        in_specs=placed,
        out_specs=(
            P(None, ("parts", "rows"), "head", None),
            P(("parts", "rows"), "head", None, None),
        ),
        check_vma=False,
    )
```

```python
import functools

import jax
import jax.numpy as jnp
from jax import lax
from jax.experimental import pallas as pl
from jax.experimental.pallas import tpu as pltpu
from jax.sharding import PartitionSpec as P

HEADS = 128
GROUPS = 4
F32 = jnp.float32
BF16 = jnp.bfloat16
VMEM = pl.BlockSpec(memory_space=pltpu.VMEM)
SMEM = pl.BlockSpec(memory_space=pltpu.SMEM)
ANY = pl.BlockSpec(memory_space=pl.ANY)


def gather_kernel(group, slots_ref, held_ref, *out_refs):
    for k, out_ref in enumerate(out_refs):
        rows = out_ref.shape[0]

        def one(r):
            out_ref[r] = held_ref[slots_ref[k * rows + r], group]

        if rows <= 16:
            for r in range(rows):
                one(r)
        else:
            pl.loop(0, rows)(one)


def gather_pieces(group, slots, held, parts):
    shape = (slots.shape[0] // parts,) + held.shape[2:]
    return pl.pallas_call(
        functools.partial(gather_kernel, group),
        in_specs=[SMEM, VMEM],
        out_specs=[VMEM] * parts,
        out_shape=[jax.ShapeDtypeStruct(shape, held.dtype)] * parts,
        compiler_params=pltpu.CompilerParams(vmem_limit_bytes=4 * 1024 * 1024),
    )(slots, held)


def split_terms(value):
    terms = []
    for _ in range(3):
        head = value.astype(BF16).astype(F32)
        terms.append(head)
        value = value - head
    return terms


def prepare_kernel(
    rows, x_ref, z_ref, dt_ref, b_ref, c_ref, head_ref,
    base_ref, carry_ref, gate_ref, left_ref, right_ref, seen_ref,
):
    both, flat = x_ref.shape
    steps = both // rows
    groups = b_ref.shape[0]
    entries = b_ref.shape[2]
    width = flat // groups
    row = lax.broadcasted_iota(jnp.int32, (both, 1), 0)

    def earlier(value, by):
        return value if by == 0 else pltpu.roll(value, by * rows, 0)

    x = x_ref[...].astype(F32)
    z = z_ref[...].astype(F32)
    gate_ref[...] = z / (1.0 + jnp.exp(-z))
    rate, bias, skip = head_ref[0:1], head_ref[1:2], head_ref[2:3]
    logit = dt_ref[...] + bias
    delta = jnp.maximum(logit, 0.0) + jnp.log1p(jnp.exp(-jnp.abs(logit)))
    kept = jnp.exp(-rate * delta)
    carry = kept
    later = jnp.where(row < both - rows, pltpu.roll(kept, both - rows, 0), 1.0)
    reach = 1
    rest = later
    while reach < steps:
        carry = carry * jnp.where(row >= reach * rows, earlier(carry, reach), 1.0)
        rest = rest * jnp.where(
            row < both - reach * rows, pltpu.roll(rest, both - reach * rows, 0), 1.0)
        reach *= 2
    carry_ref[...] = carry

    base = skip * x
    weight = jnp.ones_like(kept)
    for by in range(steps):
        if by:
            weight = weight * earlier(kept, by - 1)
        term = weight * earlier(delta, by) * earlier(x, by)
        parts = []
        for g in range(groups):
            b = b_ref[g].astype(F32)
            c = c_ref[g].astype(F32)
            match = jnp.sum(c * earlier(b, by), axis=1, keepdims=True)
            parts.append(match * term[:, g * width:(g + 1) * width])
        total = jnp.concatenate(parts, axis=1)
        base = base + jnp.where(row >= by * rows, total, 0.0)
    base_ref[...] = base

    left = split_terms(delta * rest * x) + split_terms(carry)
    left_ref[...] = jnp.concatenate(left, axis=0).astype(BF16)
    none = jnp.zeros((3 * both, entries), F32)
    for g in range(groups):
        b = b_ref[g].astype(F32)
        c = c_ref[g].astype(F32)
        right, seen = [], []
        for r in range(rows):
            mine = row % rows == r
            last = jnp.where(row == both - rows + r, 1.0, 0.0) + jnp.zeros((both, entries), F32)
            picked = jnp.where(mine, b, 0.0)
            right.append(jnp.concatenate([picked] * 3 + [none], axis=0))
            right.append(jnp.concatenate([none] + [last] * 3, axis=0))
            seen.append(jnp.where(mine, c, 0.0))
        right_ref[g] = jnp.concatenate(right, axis=1).astype(BF16)
        seen_ref[g] = jnp.concatenate(seen, axis=1).astype(BF16)


def prepare(x_new, z_gate, dt_raw, b_in, c_in, a_rate, dt_bias, skip_d):
    steps, rows, heads, channels = x_new.shape
    groups, entries = b_in.shape[2:]
    flat = heads * channels
    both = steps * rows

    def over_channels(value):
        return jnp.broadcast_to(value[..., None], value.shape + (channels,)).reshape(
            value.shape[0], flat)

    def wide(*shape):
        return jax.ShapeDtypeStruct(shape, F32 if len(shape) == 2 else BF16)

    return pl.pallas_call(
        functools.partial(prepare_kernel, rows),
        in_specs=[VMEM] * 6,
        out_specs=[VMEM] * 6,
        out_shape=[
            wide(both, flat), wide(both, flat), wide(both, flat),
            jax.ShapeDtypeStruct((6 * both, flat), BF16),
            wide(groups, 6 * both, 2 * rows * entries),
            wide(groups, both, rows * entries),
        ],
        compiler_params=pltpu.CompilerParams(vmem_limit_bytes=8 * 1024 * 1024),
    )(
        x_new.reshape(both, flat), z_gate.reshape(both, flat),
        over_channels(dt_raw.reshape(both, heads)),
        jnp.moveaxis(b_in, 2, 0).reshape(groups, both, entries),
        jnp.moveaxis(c_in, 2, 0).reshape(groups, both, entries),
        over_channels(jnp.stack([a_rate, dt_bias, skip_d])),
    )


def decode_kernel(rows, group, parts, info_ref, *refs):
    recv_refs, refs = refs[:parts], refs[parts:]
    (resident_ref, base_ref, carry_ref, gate_ref, left_ref, right_ref, seen_ref,
     gain_ref) = refs[:8]
    decoded_ref, final_ref, ready, seen, out_sem = refs[-5:]
    span, entries = recv_refs[0].shape[1:]
    block = parts * span
    start = group * block
    lanes = slice(start, start + block)

    def place(p, r):
        return pl.multiple_of((info_ref[rows + r] ^ p) * span, span)

    def result(p, r):
        return pltpu.make_async_copy(
            ready.at[r, p], final_ref.at[r, pl.ds(start + place(p, r), span)],
            out_sem.at[p, r])

    for r in range(rows):
        listed = info_ref[r] == 1
        at = 2 * r * entries
        for p in range(parts):
            here = place(p, r)
            initial = jnp.where(
                listed, recv_refs[p][r], resident_ref[r, pl.ds(start + here, span)])
            moved = lax.dot_general(
                left_ref[:, pl.ds(pl.multiple_of(start + here, span), span)],
                right_ref[group, :, at:at + 2 * entries],
                (((0,), (0,)), ((), ())), preferred_element_type=F32)
            ready[r, p] = (
                moved[:, entries:] * initial.astype(F32) + moved[:, :entries]).astype(BF16)
            result(p, r).start()
            part = lax.dot_general(
                seen_ref[group, :, r * entries:(r + 1) * entries], initial,
                (((1,), (1,)), ((), ())), preferred_element_type=F32)
            seen[r, :, pl.ds(here, span)] = part
    total = seen[0]
    for r in range(1, rows):
        total = total + seen[r]
    readout = carry_ref[:, lanes] * total + base_ref[:, lanes]
    gated = readout * gate_ref[:, lanes]
    squares = jnp.mean(gated * gated, axis=1, keepdims=True)
    normed = gated * lax.rsqrt(squares + 1e-05) * gain_ref[:, lanes]
    if group:
        decoded_ref[:, :start] = refs[8][...]
    decoded_ref[:, lanes] = normed.astype(BF16)
    for r in range(rows):
        for p in range(parts):
            result(p, r).wait()


def decode(group, info, recv, resident, ready, gain, earlier):
    rows, flat, entries = resident.shape
    both = ready[0].shape[0]
    groups = ready[4].shape[0]
    block = flat // groups
    parts, span = len(recv), block // len(recv)
    count = 1 + parts + 1 + len(ready) + 1
    return pl.pallas_call(
        functools.partial(decode_kernel, rows, group, parts),
        in_specs=[SMEM] + [VMEM] * (count - 1) + [VMEM, ANY][:len(earlier)],
        out_specs=[VMEM, ANY],
        input_output_aliases={count + 1: 1} if earlier else {},
        scratch_shapes=[
            pltpu.VMEM((rows, parts, span, entries), BF16),
            pltpu.VMEM((rows, both, block), F32),
            pltpu.SemaphoreType.DMA((parts, rows)),
        ],
        out_shape=[
            jax.ShapeDtypeStruct((both, (group + 1) * block), BF16),
            jax.ShapeDtypeStruct((rows, flat, entries), BF16),
        ],
        compiler_params=pltpu.CompilerParams(vmem_limit_bytes=16 * 1024 * 1024),
    )(info, *recv, resident, *ready, gain, *earlier)


def local(
    prefill_states, src_slot, dst_slot, resident_states, x_new, z_gate, dt_raw, b_in, c_in,
    a_rate, dt_bias, skip_d, norm_gain,
):
    row_count, local_heads, channels, entries = resident_states.shape
    flat = local_heads * channels
    shards = lax.axis_size("rows")
    me = lax.axis_index("rows")
    quarter = shards // 2
    matches = jnp.arange(shards * row_count, dtype=jnp.int32)[:, None] == dst_slot[None, :]
    listed = jnp.any(matches, axis=1).astype(jnp.int32)
    source = jnp.sum(jnp.where(matches, src_slot[None, :], 0), axis=1)

    groups = local_heads // (HEADS // GROUPS)
    span = flat // quarter // groups
    half_rows = quarter * row_count
    halves = [[h * quarter + i for i in range(quarter)] for h in range(2)]

    def exchange(value, groups=None):
        return lax.all_to_all(
            value, "rows", split_axis=0, concat_axis=0, tiled=True, axis_index_groups=groups)

    def hand(value, k):
        return lax.ppermute(value, "rows", [(i, i ^ k) for i in range(shards)])

    pieces = prefill_states.reshape(groups, quarter, span, entries)
    here = jnp.arange(shards * row_count, dtype=jnp.int32) // row_count
    few = shards == 8
    recv = []
    if few:
        arrived = [pieces[:, 0]] + [
            hand(pieces[:, k % quarter], k) for k in range(1, shards)]
        held = jnp.stack(arrived)
        order = jnp.arange(quarter)[:, None] ^ (me % quarter)
        order = (order * row_count + jnp.arange(row_count)).reshape(half_rows)
        slots = lax.dynamic_slice_in_dim(
            source ^ me, (me // quarter) * half_rows, half_rows)[order]
        for g in range(groups):
            sent = gather_pieces(g, slots, held, quarter)
            recv.append([sent[0]] + [hand(sent[k], k) for k in range(1, quarter)])
        mask = (source ^ here) % quarter
    else:
        pieces = jnp.moveaxis(pieces, 0, 1)
        held = exchange(jnp.concatenate([pieces, pieces]).reshape(
            shards, groups * span, entries)).reshape(shards, groups, span, entries)
        slots = lax.dynamic_slice_in_dim(source, (me // quarter) * half_rows, half_rows)
        for g in range(groups):
            sent, = gather_pieces(g, slots, held, 1)
            sent = exchange(sent.reshape(quarter, row_count * span, entries), halves)
            sent = jnp.moveaxis(sent.reshape(quarter, row_count, span, entries), 1, 0)
            sent = sent.reshape(row_count, 4, quarter * span // 4, entries)
            recv.append([sent[:, p] for p in range(4)])
        mask = jnp.zeros_like(source)

    groups = local_heads // (HEADS // GROUPS)
    group_base = lax.axis_index("head") * groups
    ready = prepare(
        x_new, z_gate, dt_raw,
        lax.dynamic_slice_in_dim(b_in, group_base, groups, 2),
        lax.dynamic_slice_in_dim(c_in, group_base, groups, 2),
        a_rate, dt_bias, skip_d)
    info = jnp.concatenate([
        lax.dynamic_slice_in_dim(listed, me * row_count, row_count),
        lax.dynamic_slice_in_dim(mask, me * row_count, row_count)])
    resident = resident_states.reshape(row_count, flat, entries)
    outs = ()
    for g in range(groups):
        outs = decode(g, info, recv[g], resident, ready, norm_gain.reshape(1, flat), outs)
    decoded, final = outs
    return (decoded.reshape(x_new.shape), final.reshape(resident_states.shape))


def solution(mesh):
    placed = (
        P(("parts", "rows"), "head", None, None),
        P("parts"),
        P("parts"),
        P(("parts", "rows"), "head", None, None),
        P(None, ("parts", "rows"), "head", None),
        P(None, ("parts", "rows"), "head", None),
        P(None, ("parts", "rows"), "head"),
        P(None, ("parts", "rows"), None, None),
        P(None, ("parts", "rows"), None, None),
        P("head"),
        P("head"),
        P("head"),
        P("head", None),
    )
    return jax.shard_map(
        local,
        mesh=mesh,
        in_specs=placed,
        out_specs=(
            P(None, ("parts", "rows"), "head", None),
            P(("parts", "rows"), "head", None, None),
        ),
        check_vma=False,
    )
```

```python
import functools

import jax
import jax.numpy as jnp
from jax import lax
from jax.experimental import pallas as pl
from jax.experimental.pallas import tpu as pltpu
from jax.sharding import PartitionSpec as P

HEADS = 128
GROUPS = 4
F32 = jnp.float32
BF16 = jnp.bfloat16
VMEM = pl.BlockSpec(memory_space=pltpu.VMEM)
SMEM = pl.BlockSpec(memory_space=pltpu.SMEM)
ANY = pl.BlockSpec(memory_space=pl.ANY)


def gather_kernel(slots_ref, held_ref, *out_refs):
    for k, out_ref in enumerate(out_refs):
        rows = out_ref.shape[0]

        def one(r):
            out_ref[r] = held_ref[slots_ref[k * rows + r]]

        if rows <= 16:
            for r in range(rows):
                one(r)
        else:
            pl.loop(0, rows)(one)


def gather_pieces(slots, held, parts):
    shape = (slots.shape[0] // parts,) + held.shape[1:]
    return pl.pallas_call(
        gather_kernel,
        in_specs=[SMEM, VMEM],
        out_specs=[VMEM] * parts,
        out_shape=[jax.ShapeDtypeStruct(shape, held.dtype)] * parts,
        compiler_params=pltpu.CompilerParams(vmem_limit_bytes=2 * 1024 * 1024),
    )(slots, held)


def split_terms(value):
    terms = []
    for _ in range(3):
        head = value.astype(BF16).astype(F32)
        terms.append(head)
        value = value - head
    return terms


def prepare_kernel(
    rows, x_ref, z_ref, dt_ref, b_ref, c_ref, head_ref,
    base_ref, carry_ref, gate_ref, left_ref, right_ref, seen_ref,
):
    both, flat = x_ref.shape
    steps = both // rows
    groups = b_ref.shape[0]
    entries = b_ref.shape[2]
    width = flat // groups
    row = lax.broadcasted_iota(jnp.int32, (both, 1), 0)

    def earlier(value, by):
        return value if by == 0 else pltpu.roll(value, by * rows, 0)

    x = x_ref[...].astype(F32)
    z = z_ref[...].astype(F32)
    gate_ref[...] = z / (1.0 + jnp.exp(-z))
    rate, bias, skip = head_ref[0:1], head_ref[1:2], head_ref[2:3]
    logit = dt_ref[...] + bias
    delta = jnp.maximum(logit, 0.0) + jnp.log1p(jnp.exp(-jnp.abs(logit)))
    kept = jnp.exp(-rate * delta)
    carry = kept
    later = jnp.where(row < both - rows, pltpu.roll(kept, both - rows, 0), 1.0)
    reach = 1
    rest = later
    while reach < steps:
        carry = carry * jnp.where(row >= reach * rows, earlier(carry, reach), 1.0)
        rest = rest * jnp.where(
            row < both - reach * rows, pltpu.roll(rest, both - reach * rows, 0), 1.0)
        reach *= 2
    carry_ref[...] = carry

    base = skip * x
    weight = jnp.ones_like(kept)
    for by in range(steps):
        if by:
            weight = weight * earlier(kept, by - 1)
        term = weight * earlier(delta, by) * earlier(x, by)
        parts = []
        for g in range(groups):
            b = b_ref[g].astype(F32)
            c = c_ref[g].astype(F32)
            match = jnp.sum(c * earlier(b, by), axis=1, keepdims=True)
            parts.append(match * term[:, g * width:(g + 1) * width])
        total = jnp.concatenate(parts, axis=1)
        base = base + jnp.where(row >= by * rows, total, 0.0)
    base_ref[...] = base

    left = split_terms(delta * rest * x) + split_terms(carry)
    left_ref[...] = jnp.concatenate(left, axis=0).astype(BF16)
    none = jnp.zeros((3 * both, entries), F32)
    for g in range(groups):
        b = b_ref[g].astype(F32)
        c = c_ref[g].astype(F32)
        right, seen = [], []
        for r in range(rows):
            mine = row % rows == r
            last = jnp.where(row == both - rows + r, 1.0, 0.0) + jnp.zeros((both, entries), F32)
            picked = jnp.where(mine, b, 0.0)
            right.append(jnp.concatenate([picked] * 3 + [none], axis=0))
            right.append(jnp.concatenate([none] + [last] * 3, axis=0))
            seen.append(jnp.where(mine, c, 0.0))
        right_ref[g] = jnp.concatenate(right, axis=1).astype(BF16)
        seen_ref[g] = jnp.concatenate(seen, axis=1).astype(BF16)


def prepare(x_new, z_gate, dt_raw, b_in, c_in, a_rate, dt_bias, skip_d):
    steps, rows, heads, channels = x_new.shape
    groups, entries = b_in.shape[2:]
    flat = heads * channels
    both = steps * rows

    def over_channels(value):
        return jnp.broadcast_to(value[..., None], value.shape + (channels,)).reshape(
            value.shape[0], flat)

    def wide(*shape):
        return jax.ShapeDtypeStruct(shape, F32 if len(shape) == 2 else BF16)

    return pl.pallas_call(
        functools.partial(prepare_kernel, rows),
        in_specs=[VMEM] * 6,
        out_specs=[VMEM] * 6,
        out_shape=[
            wide(both, flat), wide(both, flat), wide(both, flat),
            jax.ShapeDtypeStruct((6 * both, flat), BF16),
            wide(groups, 6 * both, 2 * rows * entries),
            wide(groups, both, rows * entries),
        ],
        compiler_params=pltpu.CompilerParams(vmem_limit_bytes=4 * 1024 * 1024),
    )(
        x_new.reshape(both, flat), z_gate.reshape(both, flat),
        over_channels(dt_raw.reshape(both, heads)),
        jnp.moveaxis(b_in, 2, 0).reshape(groups, both, entries),
        jnp.moveaxis(c_in, 2, 0).reshape(groups, both, entries),
        over_channels(jnp.stack([a_rate, dt_bias, skip_d])),
    )


def decode_kernel(rows, groups, parts, last, info_ref, *refs):
    recv_refs, refs = refs[:len(parts)], refs[len(parts):]
    left_ref, right_ref, seen_ref = refs[:3]
    span, entries = recv_refs[0].shape[2:]
    if last:
        base_ref, carry_ref, gate_ref, gain_ref, before_ref = refs[3:8]
        decoded_ref, final_ref, ready, seen, out_sem = refs[-5:]
        seen[...] = before_ref[...]
    else:
        resident_ref = refs[3]
        final_ref, seen, ready, out_sem, stay, in_sem = refs[-6:]
        seen[...] = jnp.zeros_like(seen)
    block = final_ref.shape[1] // groups
    quarters = block // span

    def advance(r, g, initial, slot, at):
        column = 2 * r * entries
        here = pl.ds(at, span)
        moved = lax.dot_general(
            left_ref[:, here], right_ref[g, :, column:column + 2 * entries],
            (((0,), (0,)), ((), ())), preferred_element_type=F32)
        ready[slot, r, g] = (
            moved[:, entries:] * initial.astype(F32) + moved[:, :entries]).astype(BF16)
        seen[r, :, here] = lax.dot_general(
            seen_ref[g, :, r * entries:(r + 1) * entries], initial,
            (((1,), (1,)), ((), ())), preferred_element_type=F32)
        return pltpu.make_async_copy(
            ready.at[slot, r, g], final_ref.at[r, here], out_sem.at[slot, r, g])

    def place(r, g, quarter):
        return pl.multiple_of(g * block + quarter * span, span)

    def listed_row(r, act):
        for p, part in enumerate(parts):
            for g in range(groups):
                act(p, g, place(r, g, info_ref[rows + r] ^ part))

    def staying_row(r, act):
        for quarter in range(quarters):
            for g in range(groups):
                act(quarter, g, place(r, g, quarter))

    def stays(r):
        return pltpu.make_async_copy(resident_ref.at[r], stay.at[r], in_sem.at[r])

    def written(r, slot, g, at):
        return pltpu.make_async_copy(
            ready.at[slot, r, g], final_ref.at[r, pl.ds(at, span)], out_sem.at[slot, r, g])

    for r in range(rows):
        if not last:

            @pl.when(info_ref[r] == 0)
            def _():
                stays(r).start()

    for r in range(rows):

        @pl.when(info_ref[r] == 1)
        def _():
            listed_row(r, lambda p, g, at: advance(r, g, recv_refs[p][r, g], p, at).start())

        if not last:

            @pl.when(info_ref[r] == 0)
            def _():
                stays(r).wait()
                staying_row(r, lambda quarter, g, at: advance(
                    r, g, stay[r, pl.ds(at, span)], quarter, at).start())

    if last:
        for g in range(groups):
            lanes = slice(g * block, (g + 1) * block)
            total = seen[0, :, lanes]
            for r in range(1, rows):
                total = total + seen[r, :, lanes]
            readout = carry_ref[:, lanes] * total + base_ref[:, lanes]
            gated = readout * gate_ref[:, lanes]
            squares = jnp.mean(gated * gated, axis=1, keepdims=True)
            normed = gated * lax.rsqrt(squares + 1e-05) * gain_ref[:, lanes]
            decoded_ref[:, lanes] = normed.astype(BF16)
    for r in range(rows):

        @pl.when(info_ref[r] == 1)
        def _():
            listed_row(r, lambda p, g, at: written(r, p, g, at).wait())

        if not last:

            @pl.when(info_ref[r] == 0)
            def _():
                staying_row(r, lambda quarter, g, at: written(r, quarter, g, at).wait())


def decode(parts, info, recv, resident, ready, gain, earlier):
    rows, flat, entries = resident.shape
    groups, span = recv[0].shape[1:3]
    base, carry, gate, left, right, seen = ready
    both = base.shape[0]
    last = len(earlier) > 0
    operands = [info, *recv, left, right, seen]
    operands += [base, carry, gate, gain, *earlier] if last else [resident]
    slots = len(parts) if last else flat // groups // span
    final = jax.ShapeDtypeStruct((rows, flat, entries), BF16)
    return pl.pallas_call(
        functools.partial(decode_kernel, rows, groups, parts, last),
        in_specs=[SMEM] + [VMEM] * (len(operands) - 2) + [ANY],
        out_specs=[VMEM, ANY] if last else [ANY, VMEM],
        input_output_aliases={len(operands) - 1: 1} if last else {},
        scratch_shapes=[pltpu.VMEM((slots, rows, groups, span, entries), BF16)]
        + [pltpu.VMEM((rows, both, flat), F32)] * last
        + [pltpu.SemaphoreType.DMA((slots, rows, groups))]
        + ([] if last else [
            pltpu.VMEM((rows, flat, entries), BF16), pltpu.SemaphoreType.DMA((rows,))]),
        out_shape=[jax.ShapeDtypeStruct((both, flat), BF16), final] if last
        else [final, jax.ShapeDtypeStruct((rows, both, flat), F32)],
        compiler_params=pltpu.CompilerParams(vmem_limit_bytes=8 * 1024 * 1024),
    )(*operands)


def local(
    prefill_states, src_slot, dst_slot, resident_states, x_new, z_gate, dt_raw, b_in, c_in,
    a_rate, dt_bias, skip_d, norm_gain,
):
    row_count, local_heads, channels, entries = resident_states.shape
    flat = local_heads * channels
    shards = lax.axis_size("rows")
    me = lax.axis_index("rows")
    quarter = shards // 2
    matches = jnp.arange(shards * row_count, dtype=jnp.int32)[:, None] == dst_slot[None, :]
    listed = jnp.any(matches, axis=1).astype(jnp.int32)
    source = jnp.sum(jnp.where(matches, src_slot[None, :], 0), axis=1)

    groups = local_heads // (HEADS // GROUPS)
    span = flat // quarter // groups
    half_rows = quarter * row_count
    halves = [[h * quarter + i for i in range(quarter)] for h in range(2)]

    def exchange(value, groups=None):
        return lax.all_to_all(
            value, "rows", split_axis=0, concat_axis=0, tiled=True, axis_index_groups=groups)

    def hand(value, k):
        return lax.ppermute(value, "rows", [(i, i ^ k) for i in range(shards)])

    pieces = prefill_states.reshape(groups, quarter, span, entries)
    here = jnp.arange(shards * row_count, dtype=jnp.int32) // row_count
    few = shards == 8
    if few:
        arrived = [pieces[:, 0]] + [
            hand(pieces[:, k % quarter], k) for k in range(1, shards)]
        held = jnp.stack(arrived)
        order = jnp.arange(quarter)[:, None] ^ (me % quarter)
        order = (order * row_count + jnp.arange(row_count)).reshape(half_rows)
        slots = lax.dynamic_slice_in_dim(
            source ^ me, (me // quarter) * half_rows, half_rows)[order]
        sent = gather_pieces(slots, held, quarter)
        recv = [sent[0]] + [hand(sent[k], k) for k in range(1, quarter)]
        mask = (source ^ here) % quarter
    else:
        pieces = jnp.moveaxis(pieces, 0, 1)
        held = exchange(jnp.concatenate([pieces, pieces]).reshape(
            shards, groups * span, entries)).reshape(shards, groups, span, entries)
        slots = lax.dynamic_slice_in_dim(source, (me // quarter) * half_rows, half_rows)
        sent, = gather_pieces(slots, held, 1)
        sent = exchange(sent.reshape(quarter, row_count * groups * span, entries), halves)
        sent = jnp.moveaxis(sent.reshape(quarter, row_count, groups, span, entries), 0, 2)
        sent = sent.reshape(row_count, groups, 4, quarter * span // 4, entries)
        recv = [sent[:, :, p] for p in range(4)]
        mask = jnp.zeros_like(source)

    groups = local_heads // (HEADS // GROUPS)
    group_base = lax.axis_index("head") * groups
    ready = prepare(
        x_new, z_gate, dt_raw,
        lax.dynamic_slice_in_dim(b_in, group_base, groups, 2),
        lax.dynamic_slice_in_dim(c_in, group_base, groups, 2),
        a_rate, dt_bias, skip_d)
    info = jnp.concatenate([
        lax.dynamic_slice_in_dim(listed, me * row_count, row_count),
        lax.dynamic_slice_in_dim(mask, me * row_count, row_count)])
    resident = resident_states.reshape(row_count, flat, entries)
    gain = norm_gain.reshape(1, flat)
    final, seen = decode((0, 1, 2), info, recv[:3], resident, ready, gain, ())
    decoded, final = decode((3,), info, recv[3:], resident, ready, gain, (seen, final))
    return (decoded.reshape(x_new.shape), final.reshape(resident_states.shape))


def solution(mesh):
    placed = (
        P(("parts", "rows"), "head", None, None),
        P("parts"),
        P("parts"),
        P(("parts", "rows"), "head", None, None),
        P(None, ("parts", "rows"), "head", None),
        P(None, ("parts", "rows"), "head", None),
        P(None, ("parts", "rows"), "head"),
        P(None, ("parts", "rows"), None, None),
        P(None, ("parts", "rows"), None, None),
        P("head"),
        P("head"),
        P("head"),
        P("head", None),
    )
    return jax.shard_map(
        local,
        mesh=mesh,
        in_specs=placed,
        out_specs=(
            P(None, ("parts", "rows"), "head", None),
            P(("parts", "rows"), "head", None, None),
        ),
        check_vma=False,
    )
```

```python
import functools

import jax
import jax.numpy as jnp
from jax import lax
from jax.experimental import pallas as pl
from jax.experimental.pallas import tpu as pltpu
from jax.sharding import PartitionSpec as P

HEADS = 128
GROUPS = 4
F32 = jnp.float32
BF16 = jnp.bfloat16
VMEM = pl.BlockSpec(memory_space=pltpu.VMEM)
SMEM = pl.BlockSpec(memory_space=pltpu.SMEM)
ANY = pl.BlockSpec(memory_space=pl.ANY)


def gather_kernel(slots_ref, held_ref, *out_refs):
    for k, out_ref in enumerate(out_refs):
        rows = out_ref.shape[0]

        def one(r):
            out_ref[r] = held_ref[slots_ref[k * rows + r]]

        if rows <= 16:
            for r in range(rows):
                one(r)
        else:
            pl.loop(0, rows)(one)


def gather_pieces(slots, held, parts):
    shape = (slots.shape[0] // parts,) + held.shape[1:]
    return pl.pallas_call(
        gather_kernel,
        in_specs=[SMEM, VMEM],
        out_specs=[VMEM] * parts,
        out_shape=[jax.ShapeDtypeStruct(shape, held.dtype)] * parts,
        compiler_params=pltpu.CompilerParams(vmem_limit_bytes=2 * 1024 * 1024),
    )(slots, held)


def split_terms(value):
    terms = []
    for _ in range(3):
        head = value.astype(BF16).astype(F32)
        terms.append(head)
        value = value - head
    return terms


def prepare_kernel(
    rows, x_ref, z_ref, dt_ref, b_ref, c_ref, head_ref,
    base_ref, carry_ref, gate_ref, left_ref, right_ref, seen_ref, head_of_ref, channel_of_ref,
):
    both, flat = x_ref.shape
    steps = both // rows
    groups = b_ref.shape[0]
    entries = b_ref.shape[2]
    width = flat // groups
    row = lax.broadcasted_iota(jnp.int32, (both, 1), 0)
    heads, channels = head_of_ref.shape[1], channel_of_ref.shape[0]
    lane = lax.broadcasted_iota(jnp.int32, (flat, heads), 0)
    first = lax.broadcasted_iota(jnp.int32, (flat, heads), 1) * channels
    inside = (lane >= first) & (lane < first + channels)
    head_of_ref[...] = jnp.where(inside, 1.0, 0.0).astype(BF16)
    lane = lax.broadcasted_iota(jnp.int32, (channels, flat), 1) % channels
    channel = lax.broadcasted_iota(jnp.int32, (channels, flat), 0)
    channel_of_ref[...] = jnp.where(lane == channel, 1.0, 0.0).astype(BF16)

    def earlier(value, by):
        return value if by == 0 else pltpu.roll(value, by * rows, 0)

    x = x_ref[...].astype(F32)
    z = z_ref[...].astype(F32)
    gate_ref[...] = z / (1.0 + jnp.exp(-z))
    rate, bias, skip = head_ref[0:1], head_ref[1:2], head_ref[2:3]
    logit = dt_ref[...] + bias
    delta = jnp.maximum(logit, 0.0) + jnp.log1p(jnp.exp(-jnp.abs(logit)))
    kept = jnp.exp(-rate * delta)
    carry = kept
    later = jnp.where(row < both - rows, pltpu.roll(kept, both - rows, 0), 1.0)
    reach = 1
    rest = later
    while reach < steps:
        carry = carry * jnp.where(row >= reach * rows, earlier(carry, reach), 1.0)
        rest = rest * jnp.where(
            row < both - reach * rows, pltpu.roll(rest, both - reach * rows, 0), 1.0)
        reach *= 2
    carry_ref[...] = carry

    base = skip * x
    weight = jnp.ones_like(kept)
    for by in range(steps):
        if by:
            weight = weight * earlier(kept, by - 1)
        term = weight * earlier(delta, by) * earlier(x, by)
        parts = []
        for g in range(groups):
            b = b_ref[g].astype(F32)
            c = c_ref[g].astype(F32)
            match = jnp.sum(c * earlier(b, by), axis=1, keepdims=True)
            parts.append(match * term[:, g * width:(g + 1) * width])
        total = jnp.concatenate(parts, axis=1)
        base = base + jnp.where(row >= by * rows, total, 0.0)
    base_ref[...] = base

    left = split_terms(delta * rest * x) + split_terms(carry)
    left_ref[...] = jnp.concatenate(left, axis=0).astype(BF16)
    none = jnp.zeros((3 * both, entries), F32)
    for g in range(groups):
        b = b_ref[g].astype(F32)
        c = c_ref[g].astype(F32)
        right, seen = [], []
        for r in range(rows):
            mine = row % rows == r
            last = jnp.where(row == both - rows + r, 1.0, 0.0) + jnp.zeros((both, entries), F32)
            picked = jnp.where(mine, b, 0.0)
            right.append(jnp.concatenate([picked] * 3 + [none], axis=0))
            right.append(jnp.concatenate([none] + [last] * 3, axis=0))
            seen.append(jnp.where(mine, c, 0.0))
        right_ref[g] = jnp.concatenate(right, axis=1).astype(BF16)
        seen_ref[g] = jnp.concatenate(seen, axis=1).astype(BF16)


def prepare(x_new, z_gate, dt_raw, b_in, c_in, a_rate, dt_bias, skip_d):
    steps, rows, heads, channels = x_new.shape
    groups, entries = b_in.shape[2:]
    flat = heads * channels
    both = steps * rows

    def over_channels(value):
        return jnp.broadcast_to(value[..., None], value.shape + (channels,)).reshape(
            value.shape[0], flat)

    def wide(*shape):
        return jax.ShapeDtypeStruct(shape, F32 if len(shape) == 2 else BF16)

    return pl.pallas_call(
        functools.partial(prepare_kernel, rows),
        in_specs=[VMEM] * 6,
        out_specs=[VMEM] * 8,
        out_shape=[
            wide(both, flat), wide(both, flat), wide(both, flat),
            jax.ShapeDtypeStruct((6 * both, flat), BF16),
            wide(groups, 6 * both, 2 * rows * entries),
            wide(groups, both, rows * entries),
            jax.ShapeDtypeStruct((flat, heads), BF16),
            jax.ShapeDtypeStruct((channels, flat), BF16),
        ],
        compiler_params=pltpu.CompilerParams(vmem_limit_bytes=4 * 1024 * 1024),
    )(
        x_new.reshape(both, flat), z_gate.reshape(both, flat),
        over_channels(dt_raw.reshape(both, heads)),
        jnp.moveaxis(b_in, 2, 0).reshape(groups, both, entries),
        jnp.moveaxis(c_in, 2, 0).reshape(groups, both, entries),
        over_channels(jnp.stack([a_rate, dt_bias, skip_d])),
    )


def decode_kernel(rows, groups, parts, last, info_ref, *refs):
    recv_refs, refs = refs[:len(parts)], refs[len(parts):]
    left_ref, right_ref, seen_ref = refs[:3]
    span, entries = recv_refs[0].shape[2:]
    if last:
        (base_ref, carry_ref, gate_ref, gain_ref, head_of_ref, channel_of_ref,
         before_ref) = refs[3:10]
        decoded_ref, final_ref, ready, seen, out_sem, turned, turn_sem = refs[-7:]
        seen[...] = before_ref[...]
    else:
        resident_ref = refs[3]
        final_ref, seen, ready, out_sem, stay, in_sem = refs[-6:]
        seen[...] = jnp.zeros_like(seen)
    block = final_ref.shape[1] // groups
    quarters = block // span

    def advance(r, g, initial, slot, at):
        column = 2 * r * entries
        here = pl.ds(at, span)
        moved = lax.dot_general(
            left_ref[:, here], right_ref[g, :, column:column + 2 * entries],
            (((0,), (0,)), ((), ())), preferred_element_type=F32)
        ready[slot, r, g] = (
            moved[:, entries:] * initial.astype(F32) + moved[:, :entries]).astype(BF16)
        seen[r, :, here] = lax.dot_general(
            seen_ref[g, :, r * entries:(r + 1) * entries], initial,
            (((1,), (1,)), ((), ())), preferred_element_type=F32)
        return pltpu.make_async_copy(
            ready.at[slot, r, g], final_ref.at[r, here], out_sem.at[slot, r, g])

    def place(r, g, quarter):
        return pl.multiple_of(g * block + quarter * span, span)

    def listed_row(r, act):
        for p, part in enumerate(parts):
            for g in range(groups):
                act(p, g, place(r, g, info_ref[rows + r] ^ part))

    def staying_row(r, act):
        for quarter in range(quarters):
            for g in range(groups):
                act(quarter, g, place(r, g, quarter))

    def stays(r):
        return pltpu.make_async_copy(resident_ref.at[r], stay.at[r], in_sem.at[r])

    def written(r, slot, g, at):
        return pltpu.make_async_copy(
            ready.at[slot, r, g], final_ref.at[r, pl.ds(at, span)], out_sem.at[slot, r, g])

    for r in range(rows):
        if not last:

            @pl.when(info_ref[r] == 0)
            def _():
                stays(r).start()

    for r in range(rows):

        @pl.when(info_ref[r] == 1)
        def _():
            listed_row(r, lambda p, g, at: advance(r, g, recv_refs[p][r, g], p, at).start())

        if not last:

            @pl.when(info_ref[r] == 0)
            def _():
                stays(r).wait()
                staying_row(r, lambda quarter, g, at: advance(
                    r, g, stay[r, pl.ds(at, span)], quarter, at).start())

    if last:
        normed = []
        for g in range(groups):
            lanes = slice(g * block, (g + 1) * block)
            total = seen[0, :, lanes]
            for r in range(1, rows):
                total = total + seen[r, :, lanes]
            readout = carry_ref[:, lanes] * total + base_ref[:, lanes]
            gated = readout * gate_ref[:, lanes]
            squares = jnp.mean(gated * gated, axis=1, keepdims=True)
            normed.append(gated * lax.rsqrt(squares + 1e-05) * gain_ref[:, lanes])
        normed = jnp.concatenate(normed, axis=1)
        both, flat = normed.shape
        channels = channel_of_ref.shape[0]
        spread = jnp.broadcast_to(normed[:, None], (both, channels, flat)).astype(BF16)
        spread = spread * channel_of_ref[...][None]
        turned[...] = jnp.dot(
            spread.reshape(both * channels, flat), head_of_ref[...],
            preferred_element_type=F32).astype(BF16).reshape(turned.shape)
        turn = pltpu.make_async_copy(turned, decoded_ref, turn_sem)
        turn.start()
    for r in range(rows):

        @pl.when(info_ref[r] == 1)
        def _():
            listed_row(r, lambda p, g, at: written(r, p, g, at).wait())

        if not last:

            @pl.when(info_ref[r] == 0)
            def _():
                staying_row(r, lambda quarter, g, at: written(r, quarter, g, at).wait())
    if last:
        turn.wait()


def decode(parts, info, recv, resident, ready, gain, earlier):
    rows, flat, entries = resident.shape
    groups, span = recv[0].shape[1:3]
    base, carry, gate, left, right, seen, head_of, channel_of = ready
    both = base.shape[0]
    last = len(earlier) > 0
    operands = [info, *recv, left, right, seen]
    operands += (
        [base, carry, gate, gain, head_of, channel_of, *earlier] if last else [resident])
    turned = (both, channel_of.shape[0], head_of.shape[1])
    slots = len(parts) if last else flat // groups // span
    final = jax.ShapeDtypeStruct((rows, flat, entries), BF16)
    return pl.pallas_call(
        functools.partial(decode_kernel, rows, groups, parts, last),
        in_specs=[SMEM] + [VMEM] * (len(operands) - 2) + [ANY],
        out_specs=[ANY, ANY] if last else [ANY, VMEM],
        input_output_aliases={len(operands) - 1: 1} if last else {},
        scratch_shapes=[pltpu.VMEM((slots, rows, groups, span, entries), BF16)]
        + [pltpu.VMEM((rows, both, flat), F32)] * last
        + [pltpu.SemaphoreType.DMA((slots, rows, groups))]
        + ([pltpu.VMEM(turned, BF16), pltpu.SemaphoreType.DMA(())] if last else [
            pltpu.VMEM((rows, flat, entries), BF16), pltpu.SemaphoreType.DMA((rows,))]),
        out_shape=[jax.ShapeDtypeStruct(turned, BF16), final] if last
        else [final, jax.ShapeDtypeStruct((rows, both, flat), F32)],
        compiler_params=pltpu.CompilerParams(vmem_limit_bytes=8 * 1024 * 1024),
    )(*operands)


def local(
    prefill_states, src_slot, dst_slot, resident_states, x_new, z_gate, dt_raw, b_in, c_in,
    a_rate, dt_bias, skip_d, norm_gain,
):
    row_count, local_heads, channels, entries = resident_states.shape
    flat = local_heads * channels
    shards = lax.axis_size("rows")
    me = lax.axis_index("rows")
    quarter = shards // 2
    matches = jnp.arange(shards * row_count, dtype=jnp.int32)[:, None] == dst_slot[None, :]
    listed = jnp.any(matches, axis=1).astype(jnp.int32)
    source = jnp.sum(jnp.where(matches, src_slot[None, :], 0), axis=1)

    groups = local_heads // (HEADS // GROUPS)
    span = flat // quarter // groups
    half_rows = quarter * row_count
    halves = [[h * quarter + i for i in range(quarter)] for h in range(2)]

    def exchange(value, groups=None):
        return lax.all_to_all(
            value, "rows", split_axis=0, concat_axis=0, tiled=True, axis_index_groups=groups)

    def hand(value, k):
        return lax.ppermute(value, "rows", [(i, i ^ k) for i in range(shards)])

    pieces = prefill_states.reshape(groups, quarter, span, entries)
    here = jnp.arange(shards * row_count, dtype=jnp.int32) // row_count
    few = shards == 8
    if few:
        first, rest = lax.optimization_barrier((pieces[:, 1], pieces))
        cut = [rest[:, 0], first, rest[:, 2], rest[:, 3]]
        arrived = [cut[0]] + [hand(cut[k % quarter], k) for k in range(1, shards)]
        held = jnp.stack(arrived)
        order = jnp.arange(quarter)[:, None] ^ (me % quarter)
        order = (order * row_count + jnp.arange(row_count)).reshape(half_rows)
        slots = lax.dynamic_slice_in_dim(
            source ^ me, (me // quarter) * half_rows, half_rows)[order]
        sent = gather_pieces(slots, held, quarter)
        recv = [sent[0]] + [hand(sent[k], k) for k in range(1, quarter)]
        mask = (source ^ here) % quarter
    else:
        pieces = jnp.moveaxis(pieces, 0, 1)
        held = exchange(jnp.concatenate([pieces, pieces]).reshape(
            shards, groups * span, entries)).reshape(shards, groups, span, entries)
        slots = lax.dynamic_slice_in_dim(source, (me // quarter) * half_rows, half_rows)
        sent, = gather_pieces(slots, held, 1)
        sent = exchange(sent.reshape(quarter, row_count * groups * span, entries), halves)
        sent = jnp.moveaxis(sent.reshape(quarter, row_count, groups, span, entries), 0, 2)
        sent = sent.reshape(row_count, groups, 4, quarter * span // 4, entries)
        recv = [sent[:, :, p] for p in range(4)]
        mask = jnp.zeros_like(source)

    groups = local_heads // (HEADS // GROUPS)
    group_base = lax.axis_index("head") * groups
    ready = prepare(
        x_new, z_gate, dt_raw,
        lax.dynamic_slice_in_dim(b_in, group_base, groups, 2),
        lax.dynamic_slice_in_dim(c_in, group_base, groups, 2),
        a_rate, dt_bias, skip_d)
    info = jnp.concatenate([
        lax.dynamic_slice_in_dim(listed, me * row_count, row_count),
        lax.dynamic_slice_in_dim(mask, me * row_count, row_count)])
    resident = resident_states.reshape(row_count, flat, entries)
    gain = norm_gain.reshape(1, flat)
    final, seen = decode((0, 1, 2), info, recv[:3], resident, ready, gain, ())
    decoded, final = decode((3,), info, recv[3:], resident, ready, gain, (seen, final))
    steps = x_new.shape[0]
    decoded = decoded.reshape(steps, row_count, channels, local_heads)
    return (jnp.swapaxes(decoded, 2, 3), final.reshape(resident_states.shape))


def solution(mesh):
    placed = (
        P(("parts", "rows"), "head", None, None),
        P("parts"),
        P("parts"),
        P(("parts", "rows"), "head", None, None),
        P(None, ("parts", "rows"), "head", None),
        P(None, ("parts", "rows"), "head", None),
        P(None, ("parts", "rows"), "head"),
        P(None, ("parts", "rows"), None, None),
        P(None, ("parts", "rows"), None, None),
        P("head"),
        P("head"),
        P("head"),
        P("head", None),
    )
    return jax.shard_map(
        local,
        mesh=mesh,
        in_specs=placed,
        out_specs=(
            P(None, ("parts", "rows"), "head", None),
            P(("parts", "rows"), "head", None, None),
        ),
        check_vma=False,
    )
```

```python
import functools

import jax
import jax.numpy as jnp
from jax import lax
from jax.experimental import pallas as pl
from jax.experimental.pallas import tpu as pltpu
from jax.sharding import PartitionSpec as P

HEADS = 128
GROUPS = 4
F32 = jnp.float32
BF16 = jnp.bfloat16
VMEM = pl.BlockSpec(memory_space=pltpu.VMEM)
SMEM = pl.BlockSpec(memory_space=pltpu.SMEM)
ANY = pl.BlockSpec(memory_space=pl.ANY)


def gather_kernel(slots_ref, held_ref, *out_refs):
    for k, out_ref in enumerate(out_refs):
        rows = out_ref.shape[0]

        def one(r):
            out_ref[r] = held_ref[slots_ref[0, k * rows + r]]

        if rows <= 16:
            for r in range(rows):
                one(r)
        else:
            pl.loop(0, rows)(one)


def gather_pieces(slots, held, parts):
    shape = (slots.shape[0] // parts,) + held.shape[1:]
    return pl.pallas_call(
        gather_kernel,
        in_specs=[VMEM if parts > 1 else SMEM, VMEM],
        out_specs=[VMEM] * parts,
        out_shape=[jax.ShapeDtypeStruct(shape, held.dtype)] * parts,
        compiler_params=pltpu.CompilerParams(vmem_limit_bytes=2 * 1024 * 1024),
    )(slots[None], held)


def split_terms(value):
    terms = []
    for _ in range(3):
        head = value.astype(BF16).astype(F32)
        terms.append(head)
        value = value - head
    return terms


def prepare_kernel(
    rows, x_ref, z_ref, dt_ref, b_ref, c_ref, head_ref,
    base_ref, carry_ref, gate_ref, left_ref, right_ref, seen_ref, head_of_ref, channel_of_ref,
):
    both, flat = x_ref.shape
    steps = both // rows
    groups = b_ref.shape[0]
    entries = b_ref.shape[2]
    width = flat // groups
    row = lax.broadcasted_iota(jnp.int32, (both, 1), 0)
    heads, channels = head_of_ref.shape[1], channel_of_ref.shape[0]
    lane = lax.broadcasted_iota(jnp.int32, (flat, heads), 0)
    first = lax.broadcasted_iota(jnp.int32, (flat, heads), 1) * channels
    inside = (lane >= first) & (lane < first + channels)
    head_of_ref[...] = jnp.where(inside, 1.0, 0.0).astype(BF16)
    lane = lax.broadcasted_iota(jnp.int32, (channels, flat), 1) % channels
    channel = lax.broadcasted_iota(jnp.int32, (channels, flat), 0)
    channel_of_ref[...] = jnp.where(lane == channel, 1.0, 0.0).astype(BF16)

    def earlier(value, by):
        return value if by == 0 else pltpu.roll(value, by * rows, 0)

    x = x_ref[...].astype(F32)
    z = z_ref[...].astype(F32)
    gate_ref[...] = z / (1.0 + jnp.exp(-z))
    rate, bias, skip = head_ref[0:1], head_ref[1:2], head_ref[2:3]
    logit = dt_ref[...] + bias
    delta = jnp.maximum(logit, 0.0) + jnp.log1p(jnp.exp(-jnp.abs(logit)))
    kept = jnp.exp(-rate * delta)
    carry = kept
    later = jnp.where(row < both - rows, pltpu.roll(kept, both - rows, 0), 1.0)
    reach = 1
    rest = later
    while reach < steps:
        carry = carry * jnp.where(row >= reach * rows, earlier(carry, reach), 1.0)
        rest = rest * jnp.where(
            row < both - reach * rows, pltpu.roll(rest, both - reach * rows, 0), 1.0)
        reach *= 2
    carry_ref[...] = carry

    base = skip * x
    weight = jnp.ones_like(kept)
    for by in range(steps):
        if by:
            weight = weight * earlier(kept, by - 1)
        term = weight * earlier(delta, by) * earlier(x, by)
        parts = []
        for g in range(groups):
            b = b_ref[g].astype(F32)
            c = c_ref[g].astype(F32)
            match = jnp.sum(c * earlier(b, by), axis=1, keepdims=True)
            parts.append(match * term[:, g * width:(g + 1) * width])
        total = jnp.concatenate(parts, axis=1)
        base = base + jnp.where(row >= by * rows, total, 0.0)
    base_ref[...] = base

    left = split_terms(delta * rest * x) + split_terms(carry)
    left_ref[...] = jnp.concatenate(left, axis=0).astype(BF16)
    none = jnp.zeros((3 * both, entries), F32)
    for g in range(groups):
        b = b_ref[g].astype(F32)
        c = c_ref[g].astype(F32)
        right, seen = [], []
        for r in range(rows):
            mine = row % rows == r
            last = jnp.where(row == both - rows + r, 1.0, 0.0) + jnp.zeros((both, entries), F32)
            picked = jnp.where(mine, b, 0.0)
            right.append(jnp.concatenate([picked] * 3 + [none], axis=0))
            right.append(jnp.concatenate([none] + [last] * 3, axis=0))
            seen.append(jnp.where(mine, c, 0.0))
        right_ref[g] = jnp.concatenate(right, axis=1).astype(BF16)
        seen_ref[g] = jnp.concatenate(seen, axis=1).astype(BF16)


def prepare(x_new, z_gate, dt_raw, b_in, c_in, a_rate, dt_bias, skip_d):
    steps, rows, heads, channels = x_new.shape
    groups, entries = b_in.shape[2:]
    flat = heads * channels
    both = steps * rows

    def over_channels(value):
        return jnp.broadcast_to(value[..., None], value.shape + (channels,)).reshape(
            value.shape[0], flat)

    def wide(*shape):
        return jax.ShapeDtypeStruct(shape, F32 if len(shape) == 2 else BF16)

    return pl.pallas_call(
        functools.partial(prepare_kernel, rows),
        in_specs=[VMEM] * 6,
        out_specs=[VMEM] * 8,
        out_shape=[
            wide(both, flat), wide(both, flat), wide(both, flat),
            jax.ShapeDtypeStruct((6 * both, flat), BF16),
            wide(groups, 6 * both, 2 * rows * entries),
            wide(groups, both, rows * entries),
            jax.ShapeDtypeStruct((flat, heads), BF16),
            jax.ShapeDtypeStruct((channels, flat), BF16),
        ],
        compiler_params=pltpu.CompilerParams(vmem_limit_bytes=4 * 1024 * 1024),
    )(
        x_new.reshape(both, flat), z_gate.reshape(both, flat),
        over_channels(dt_raw.reshape(both, heads)),
        jnp.moveaxis(b_in, 2, 0).reshape(groups, both, entries),
        jnp.moveaxis(c_in, 2, 0).reshape(groups, both, entries),
        over_channels(jnp.stack([a_rate, dt_bias, skip_d])),
    )


def decode_kernel(rows, groups, parts, last, info_row, *refs):
    info_ref = [info_row[0, i] for i in range(2 * rows)]
    recv_refs, refs = refs[:len(parts)], refs[len(parts):]
    left_ref, right_ref, seen_ref = refs[:3]
    span, entries = recv_refs[0].shape[2:]
    if last:
        (base_ref, carry_ref, gate_ref, gain_ref, head_of_ref, channel_of_ref,
         before_ref) = refs[3:10]
        decoded_ref, final_ref, ready, seen, out_sem, turned, turn_sem = refs[-7:]
        seen[...] = before_ref[...]
    else:
        resident_ref = refs[3]
        final_ref, seen, ready, out_sem, stay, in_sem = refs[-6:]
        seen[...] = jnp.zeros_like(seen)
    block = final_ref.shape[1] // groups
    quarters = block // span

    def advance(r, g, initial, slot, at):
        column = 2 * r * entries
        here = pl.ds(at, span)
        moved = lax.dot_general(
            left_ref[:, here], right_ref[g, :, column:column + 2 * entries],
            (((0,), (0,)), ((), ())), preferred_element_type=F32)
        ready[slot, r, g] = (
            moved[:, entries:] * initial.astype(F32) + moved[:, :entries]).astype(BF16)
        seen[r, :, here] = lax.dot_general(
            seen_ref[g, :, r * entries:(r + 1) * entries], initial,
            (((1,), (1,)), ((), ())), preferred_element_type=F32)
        return pltpu.make_async_copy(
            ready.at[slot, r, g], final_ref.at[r, here], out_sem.at[slot, r, g])

    def place(r, g, quarter):
        return pl.multiple_of(g * block + quarter * span, span)

    def listed_row(r, act):
        for p, part in enumerate(parts):
            for g in range(groups):
                act(p, g, place(r, g, info_ref[rows + r] ^ part))

    def staying_row(r, act):
        for quarter in range(quarters):
            for g in range(groups):
                act(quarter, g, place(r, g, quarter))

    def stays(r):
        return pltpu.make_async_copy(resident_ref.at[r], stay.at[r], in_sem.at[r])

    def written(r, slot, g, at):
        return pltpu.make_async_copy(
            ready.at[slot, r, g], final_ref.at[r, pl.ds(at, span)], out_sem.at[slot, r, g])

    for r in range(rows):
        if not last:

            @pl.when(info_ref[r] == 0)
            def _():
                stays(r).start()

    for r in range(rows):

        @pl.when(info_ref[r] == 1)
        def _():
            listed_row(r, lambda p, g, at: advance(r, g, recv_refs[p][r, g], p, at).start())

        if not last:

            @pl.when(info_ref[r] == 0)
            def _():
                stays(r).wait()
                staying_row(r, lambda quarter, g, at: advance(
                    r, g, stay[r, pl.ds(at, span)], quarter, at).start())

    if last:
        normed = []
        for g in range(groups):
            lanes = slice(g * block, (g + 1) * block)
            total = seen[0, :, lanes]
            for r in range(1, rows):
                total = total + seen[r, :, lanes]
            readout = carry_ref[:, lanes] * total + base_ref[:, lanes]
            gated = readout * gate_ref[:, lanes]
            squares = jnp.mean(gated * gated, axis=1, keepdims=True)
            normed.append(gated * lax.rsqrt(squares + 1e-05) * gain_ref[:, lanes])
        normed = jnp.concatenate(normed, axis=1)
        both, flat = normed.shape
        channels = channel_of_ref.shape[0]
        spread = jnp.broadcast_to(normed[:, None], (both, channels, flat)).astype(BF16)
        spread = spread * channel_of_ref[...][None]
        turned[...] = jnp.dot(
            spread.reshape(both * channels, flat), head_of_ref[...],
            preferred_element_type=F32).astype(BF16).reshape(turned.shape)
        turn = pltpu.make_async_copy(turned, decoded_ref, turn_sem)
        turn.start()
    for r in range(rows):

        @pl.when(info_ref[r] == 1)
        def _():
            listed_row(r, lambda p, g, at: written(r, p, g, at).wait())

        if not last:

            @pl.when(info_ref[r] == 0)
            def _():
                staying_row(r, lambda quarter, g, at: written(r, quarter, g, at).wait())
    if last:
        turn.wait()


def decode(parts, info, recv, resident, ready, gain, earlier):
    rows, flat, entries = resident.shape
    groups, span = recv[0].shape[1:3]
    base, carry, gate, left, right, seen, head_of, channel_of = ready
    both = base.shape[0]
    last = len(earlier) > 0
    operands = [info, *recv, left, right, seen]
    operands += (
        [base, carry, gate, gain, head_of, channel_of, *earlier] if last else [resident])
    turned = (both, channel_of.shape[0], head_of.shape[1])
    slots = len(parts) if last else flat // groups // span
    final = jax.ShapeDtypeStruct((rows, flat, entries), BF16)
    return pl.pallas_call(
        functools.partial(decode_kernel, rows, groups, parts, last),
        in_specs=[VMEM] * (len(operands) - 1) + [ANY],
        out_specs=[ANY, ANY] if last else [ANY, VMEM],
        input_output_aliases={len(operands) - 1: 1} if last else {},
        scratch_shapes=[pltpu.VMEM((slots, rows, groups, span, entries), BF16)]
        + [pltpu.VMEM((rows, both, flat), F32)] * last
        + [pltpu.SemaphoreType.DMA((slots, rows, groups))]
        + ([pltpu.VMEM(turned, BF16), pltpu.SemaphoreType.DMA(())] if last else [
            pltpu.VMEM((rows, flat, entries), BF16), pltpu.SemaphoreType.DMA((rows,))]),
        out_shape=[jax.ShapeDtypeStruct(turned, BF16), final] if last
        else [final, jax.ShapeDtypeStruct((rows, both, flat), F32)],
        compiler_params=pltpu.CompilerParams(vmem_limit_bytes=8 * 1024 * 1024),
    )(*operands)


def local(
    prefill_states, src_slot, dst_slot, resident_states, x_new, z_gate, dt_raw, b_in, c_in,
    a_rate, dt_bias, skip_d, norm_gain,
):
    row_count, local_heads, channels, entries = resident_states.shape
    flat = local_heads * channels
    shards = lax.axis_size("rows")
    me = lax.axis_index("rows")
    quarter = shards // 2
    matches = jnp.arange(shards * row_count, dtype=jnp.int32)[:, None] == dst_slot[None, :]
    listed = jnp.any(matches, axis=1).astype(jnp.int32)
    source = jnp.sum(jnp.where(matches, src_slot[None, :], 0), axis=1)

    groups = local_heads // (HEADS // GROUPS)
    span = flat // quarter // groups
    half_rows = quarter * row_count
    halves = [[h * quarter + i for i in range(quarter)] for h in range(2)]

    def exchange(value, groups=None):
        return lax.all_to_all(
            value, "rows", split_axis=0, concat_axis=0, tiled=True, axis_index_groups=groups)

    def hand(value, k):
        return lax.ppermute(value, "rows", [(i, i ^ k) for i in range(shards)])

    pieces = prefill_states.reshape(groups, quarter, span, entries)
    here = jnp.arange(shards * row_count, dtype=jnp.int32) // row_count
    few = shards == 8
    if few:
        first, rest = lax.optimization_barrier((pieces[:, 1], pieces))
        cut = [rest[:, 0], first, rest[:, 2], rest[:, 3]]
        arrived = [cut[0]] + [hand(cut[k % quarter], k) for k in range(1, shards)]
        held = jnp.stack(arrived)
        order = jnp.arange(quarter)[:, None] ^ (me % quarter)
        order = (order * row_count + jnp.arange(row_count)).reshape(half_rows)
        slots = lax.dynamic_slice_in_dim(
            source ^ me, (me // quarter) * half_rows, half_rows)[order]
        sent = gather_pieces(slots, held, quarter)
        recv = [sent[0]] + [hand(sent[k], k) for k in range(1, quarter)]
        mask = (source ^ here) % quarter
    else:
        pieces = jnp.moveaxis(pieces, 0, 1)
        held = exchange(jnp.concatenate([pieces, pieces]).reshape(
            shards, groups * span, entries)).reshape(shards, groups, span, entries)
        slots = lax.dynamic_slice_in_dim(source, (me // quarter) * half_rows, half_rows)
        sent, = gather_pieces(slots, held, 1)
        sent = exchange(sent.reshape(quarter, row_count * groups * span, entries), halves)
        sent = jnp.moveaxis(sent.reshape(quarter, row_count, groups, span, entries), 0, 2)
        sent = sent.reshape(row_count, groups, 4, quarter * span // 4, entries)
        recv = [sent[:, :, p] for p in range(4)]
        mask = jnp.zeros_like(source)

    groups = local_heads // (HEADS // GROUPS)
    group_base = lax.axis_index("head") * groups
    ready = prepare(
        x_new, z_gate, dt_raw,
        lax.dynamic_slice_in_dim(b_in, group_base, groups, 2),
        lax.dynamic_slice_in_dim(c_in, group_base, groups, 2),
        a_rate, dt_bias, skip_d)
    info = jnp.concatenate([
        lax.dynamic_slice_in_dim(listed, me * row_count, row_count),
        lax.dynamic_slice_in_dim(mask, me * row_count, row_count)])[None]
    resident = resident_states.reshape(row_count, flat, entries)
    gain = norm_gain.reshape(1, flat)
    final, seen = decode((0, 1, 2), info, recv[:3], resident, ready, gain, ())
    decoded, final = decode((3,), info, recv[3:], resident, ready, gain, (seen, final))
    steps = x_new.shape[0]
    decoded = decoded.reshape(steps, row_count, channels, local_heads)
    return (jnp.swapaxes(decoded, 2, 3), final.reshape(resident_states.shape))


def solution(mesh):
    placed = (
        P(("parts", "rows"), "head", None, None),
        P("parts"),
        P("parts"),
        P(("parts", "rows"), "head", None, None),
        P(None, ("parts", "rows"), "head", None),
        P(None, ("parts", "rows"), "head", None),
        P(None, ("parts", "rows"), "head"),
        P(None, ("parts", "rows"), None, None),
        P(None, ("parts", "rows"), None, None),
        P("head"),
        P("head"),
        P("head"),
        P("head", None),
    )
    return jax.shard_map(
        local,
        mesh=mesh,
        in_specs=placed,
        out_specs=(
            P(None, ("parts", "rows"), "head", None),
            P(("parts", "rows"), "head", None, None),
        ),
        check_vma=False,
    )
```

```python
import functools

import jax
import jax.numpy as jnp
from jax import lax
from jax.experimental import pallas as pl
from jax.experimental.pallas import tpu as pltpu
from jax.sharding import PartitionSpec as P

HEADS = 128
GROUPS = 4
F32 = jnp.float32
BF16 = jnp.bfloat16
VMEM = pl.BlockSpec(memory_space=pltpu.VMEM)
SMEM = pl.BlockSpec(memory_space=pltpu.SMEM)
ANY = pl.BlockSpec(memory_space=pl.ANY)


def gather_kernel(slots_ref, held_ref, *out_refs):
    for k, out_ref in enumerate(out_refs):
        rows = out_ref.shape[0]

        def one(r):
            out_ref[r] = held_ref[slots_ref[0, k * rows + r]]

        if rows <= 16:
            for r in range(rows):
                one(r)
        else:
            pl.loop(0, rows)(one)


def gather_pieces(slots, held, parts):
    shape = (slots.shape[0] // parts,) + held.shape[1:]
    return pl.pallas_call(
        gather_kernel,
        in_specs=[VMEM if parts > 1 else SMEM, VMEM],
        out_specs=[VMEM] * parts,
        out_shape=[jax.ShapeDtypeStruct(shape, held.dtype)] * parts,
        compiler_params=pltpu.CompilerParams(vmem_limit_bytes=2 * 1024 * 1024),
    )(slots[None], held)


def split_terms(value):
    terms = []
    for _ in range(3):
        head = value.astype(BF16).astype(F32)
        terms.append(head)
        value = value - head
    return terms


def prepare_kernel(
    rows, x_ref, z_ref, dt_ref, b_ref, c_ref, head_ref,
    base_ref, carry_ref, gate_ref, left_ref, right_ref, seen_ref, head_of_ref, channel_of_ref,
):
    both, flat = x_ref.shape
    steps = both // rows
    groups = b_ref.shape[0]
    entries = b_ref.shape[2]
    width = flat // groups
    row = lax.broadcasted_iota(jnp.int32, (both, 1), 0)
    heads, channels = head_of_ref.shape[1], channel_of_ref.shape[0]
    lane = lax.broadcasted_iota(jnp.int32, (flat, heads), 0)
    first = lax.broadcasted_iota(jnp.int32, (flat, heads), 1) * channels
    inside = (lane >= first) & (lane < first + channels)
    head_of_ref[...] = jnp.where(inside, 1.0, 0.0).astype(BF16)
    lane = lax.broadcasted_iota(jnp.int32, (channels, flat), 1) % channels
    channel = lax.broadcasted_iota(jnp.int32, (channels, flat), 0)
    channel_of_ref[...] = jnp.where(lane == channel, 1.0, 0.0).astype(BF16)

    def earlier(value, by):
        return value if by == 0 else pltpu.roll(value, by * rows, 0)

    x = x_ref[...].astype(F32)
    z = z_ref[...].astype(F32)
    gate_ref[...] = z / (1.0 + jnp.exp(-z))
    rate, bias, skip = head_ref[0:1], head_ref[1:2], head_ref[2:3]
    logit = dt_ref[...] + bias
    delta = jnp.maximum(logit, 0.0) + jnp.log1p(jnp.exp(-jnp.abs(logit)))
    kept = jnp.exp(-rate * delta)
    carry = kept
    later = jnp.where(row < both - rows, pltpu.roll(kept, both - rows, 0), 1.0)
    reach = 1
    rest = later
    while reach < steps:
        carry = carry * jnp.where(row >= reach * rows, earlier(carry, reach), 1.0)
        rest = rest * jnp.where(
            row < both - reach * rows, pltpu.roll(rest, both - reach * rows, 0), 1.0)
        reach *= 2
    carry_ref[...] = carry

    base = skip * x
    weight = jnp.ones_like(kept)
    for by in range(steps):
        if by:
            weight = weight * earlier(kept, by - 1)
        term = weight * earlier(delta, by) * earlier(x, by)
        parts = []
        for g in range(groups):
            b = b_ref[g].astype(F32)
            c = c_ref[g].astype(F32)
            match = jnp.sum(c * earlier(b, by), axis=1, keepdims=True)
            parts.append(match * term[:, g * width:(g + 1) * width])
        total = jnp.concatenate(parts, axis=1)
        base = base + jnp.where(row >= by * rows, total, 0.0)
    base_ref[...] = base

    left = split_terms(delta * rest * x) + split_terms(carry)
    left_ref[...] = jnp.concatenate(left, axis=0).astype(BF16)
    none = jnp.zeros((3 * both, entries), F32)
    for g in range(groups):
        b = b_ref[g].astype(F32)
        c = c_ref[g].astype(F32)
        right, seen = [], []
        for r in range(rows):
            mine = row % rows == r
            last = jnp.where(row == both - rows + r, 1.0, 0.0) + jnp.zeros((both, entries), F32)
            picked = jnp.where(mine, b, 0.0)
            right.append(jnp.concatenate([picked] * 3 + [none], axis=0))
            right.append(jnp.concatenate([none] + [last] * 3, axis=0))
            seen.append(jnp.where(mine, c, 0.0))
        right_ref[g] = jnp.concatenate(right, axis=1).astype(BF16)
        seen_ref[g] = jnp.concatenate(seen, axis=1).astype(BF16)


def prepare(x_new, z_gate, dt_raw, b_in, c_in, a_rate, dt_bias, skip_d):
    steps, rows, heads, channels = x_new.shape
    groups, entries = b_in.shape[2:]
    flat = heads * channels
    both = steps * rows

    def over_channels(value):
        return jnp.broadcast_to(value[..., None], value.shape + (channels,)).reshape(
            value.shape[0], flat)

    def wide(*shape):
        return jax.ShapeDtypeStruct(shape, F32 if len(shape) == 2 else BF16)

    return pl.pallas_call(
        functools.partial(prepare_kernel, rows),
        in_specs=[VMEM] * 6,
        out_specs=[VMEM] * 8,
        out_shape=[
            wide(both, flat), wide(both, flat), wide(both, flat),
            jax.ShapeDtypeStruct((6 * both, flat), BF16),
            wide(groups, 6 * both, 2 * rows * entries),
            wide(groups, both, rows * entries),
            jax.ShapeDtypeStruct((flat, heads), BF16),
            jax.ShapeDtypeStruct((channels, flat), BF16),
        ],
        compiler_params=pltpu.CompilerParams(vmem_limit_bytes=4 * 1024 * 1024),
    )(
        x_new.reshape(both, flat), z_gate.reshape(both, flat),
        over_channels(dt_raw.reshape(both, heads)),
        jnp.moveaxis(b_in, 2, 0).reshape(groups, both, entries),
        jnp.moveaxis(c_in, 2, 0).reshape(groups, both, entries),
        over_channels(jnp.stack([a_rate, dt_bias, skip_d])),
    )


def decode_kernel(rows, groups, parts, last, info_row, *refs):
    info_ref = [info_row[0, i] for i in range(info_row.shape[1])]
    recv_refs, refs = refs[:len(parts)], refs[len(parts):]
    left_ref, right_ref, seen_ref = refs[:3]
    span, entries = recv_refs[0].shape[2:]
    if last:
        (base_ref, carry_ref, gate_ref, gain_ref, head_of_ref, channel_of_ref,
         before_ref) = refs[3:10]
        decoded_ref, final_ref, ready, seen, out_sem, turned, turn_sem = refs[-7:]
        seen[...] = before_ref[...]
    else:
        resident_ref = refs[3]
        final_ref, seen, ready, out_sem, stay, in_sem = refs[-6:]
        seen[...] = jnp.zeros_like(seen)
    block = final_ref.shape[1] // groups
    quarters = block // span

    def advance(r, g, initial, slot, at):
        column = 2 * r * entries
        here = pl.ds(at, span)
        moved = lax.dot_general(
            left_ref[:, here], right_ref[g, :, column:column + 2 * entries],
            (((0,), (0,)), ((), ())), preferred_element_type=F32)
        ready[slot, r, g] = (
            moved[:, entries:] * initial.astype(F32) + moved[:, :entries]).astype(BF16)
        seen[r, :, here] = lax.dot_general(
            seen_ref[g, :, r * entries:(r + 1) * entries], initial,
            (((1,), (1,)), ((), ())), preferred_element_type=F32)
        return pltpu.make_async_copy(
            ready.at[slot, r, g], final_ref.at[r, here], out_sem.at[slot, r, g])

    def place(r, g, quarter):
        return pl.multiple_of(g * block + quarter * span, span)

    def listed_row(r, act):
        for p, part in enumerate(parts):
            for g in range(groups):
                act(p, g, place(r, g, info_ref[rows + r] ^ info_ref[2 * rows + part]))

    def staying_row(r, act):
        for quarter in range(quarters):
            for g in range(groups):
                act(quarter, g, place(r, g, quarter))

    def stays(r):
        return pltpu.make_async_copy(resident_ref.at[r], stay.at[r], in_sem.at[r])

    def written(r, slot, g, at):
        return pltpu.make_async_copy(
            ready.at[slot, r, g], final_ref.at[r, pl.ds(at, span)], out_sem.at[slot, r, g])

    for r in range(rows):
        if not last:

            @pl.when(info_ref[r] == 0)
            def _():
                stays(r).start()

    for r in range(rows):

        @pl.when(info_ref[r] == 1)
        def _():
            listed_row(r, lambda p, g, at: advance(r, g, recv_refs[p][r, g], p, at).start())

        if not last:

            @pl.when(info_ref[r] == 0)
            def _():
                stays(r).wait()
                staying_row(r, lambda quarter, g, at: advance(
                    r, g, stay[r, pl.ds(at, span)], quarter, at).start())

    if last:
        normed = []
        for g in range(groups):
            lanes = slice(g * block, (g + 1) * block)
            total = seen[0, :, lanes]
            for r in range(1, rows):
                total = total + seen[r, :, lanes]
            readout = carry_ref[:, lanes] * total + base_ref[:, lanes]
            gated = readout * gate_ref[:, lanes]
            squares = jnp.mean(gated * gated, axis=1, keepdims=True)
            normed.append(gated * lax.rsqrt(squares + 1e-05) * gain_ref[:, lanes])
        normed = jnp.concatenate(normed, axis=1)
        both, flat = normed.shape
        channels = channel_of_ref.shape[0]
        spread = jnp.broadcast_to(normed[:, None], (both, channels, flat)).astype(BF16)
        spread = spread * channel_of_ref[...][None]
        turned[...] = jnp.dot(
            spread.reshape(both * channels, flat), head_of_ref[...],
            preferred_element_type=F32).astype(BF16).reshape(turned.shape)
        turn = pltpu.make_async_copy(turned, decoded_ref, turn_sem)
        turn.start()
    for r in range(rows):

        @pl.when(info_ref[r] == 1)
        def _():
            listed_row(r, lambda p, g, at: written(r, p, g, at).wait())

        if not last:

            @pl.when(info_ref[r] == 0)
            def _():
                staying_row(r, lambda quarter, g, at: written(r, quarter, g, at).wait())
    if last:
        turn.wait()


def decode(parts, info, recv, resident, ready, gain, earlier):
    rows, flat, entries = resident.shape
    groups, span = recv[0].shape[1:3]
    base, carry, gate, left, right, seen, head_of, channel_of = ready
    both = base.shape[0]
    last = len(earlier) > 0
    operands = [info, *recv, left, right, seen]
    operands += (
        [base, carry, gate, gain, head_of, channel_of, *earlier] if last else [resident])
    turned = (both, channel_of.shape[0], head_of.shape[1])
    slots = len(parts) if last else flat // groups // span
    final = jax.ShapeDtypeStruct((rows, flat, entries), BF16)
    return pl.pallas_call(
        functools.partial(decode_kernel, rows, groups, parts, last),
        in_specs=[VMEM] * (len(operands) - 1) + [ANY],
        out_specs=[ANY, ANY] if last else [ANY, VMEM],
        input_output_aliases={len(operands) - 1: 1} if last else {},
        scratch_shapes=[pltpu.VMEM((slots, rows, groups, span, entries), BF16)]
        + [pltpu.VMEM((rows, both, flat), F32)] * last
        + [pltpu.SemaphoreType.DMA((slots, rows, groups))]
        + ([pltpu.VMEM(turned, BF16), pltpu.SemaphoreType.DMA(())] if last else [
            pltpu.VMEM((rows, flat, entries), BF16), pltpu.SemaphoreType.DMA((rows,))]),
        out_shape=[jax.ShapeDtypeStruct(turned, BF16), final] if last
        else [final, jax.ShapeDtypeStruct((rows, both, flat), F32)],
        compiler_params=pltpu.CompilerParams(vmem_limit_bytes=8 * 1024 * 1024),
    )(*operands)


def local(
    prefill_states, src_slot, dst_slot, resident_states, x_new, z_gate, dt_raw, b_in, c_in,
    a_rate, dt_bias, skip_d, norm_gain,
):
    row_count, local_heads, channels, entries = resident_states.shape
    flat = local_heads * channels
    shards = lax.axis_size("rows")
    me = lax.axis_index("rows")
    quarter = shards // 2
    matches = jnp.arange(shards * row_count, dtype=jnp.int32)[:, None] == dst_slot[None, :]
    listed = jnp.any(matches, axis=1).astype(jnp.int32)
    source = jnp.sum(jnp.where(matches, src_slot[None, :], 0), axis=1)

    groups = local_heads // (HEADS // GROUPS)
    span = flat // quarter // groups
    half_rows = quarter * row_count
    halves = [[h * quarter + i for i in range(quarter)] for h in range(2)]

    def exchange(value, groups=None):
        return lax.all_to_all(
            value, "rows", split_axis=0, concat_axis=0, tiled=True, axis_index_groups=groups)

    cores = lax.axis_size("head")
    core = lax.axis_index("head")

    def hand(value, distances):
        return lax.ppermute(value, ("rows", "head"), [
            (i * cores + c, (i ^ distances[c % 2]) * cores + c)
            for i in range(shards) for c in range(cores)])

    pieces = prefill_states.reshape(groups, quarter, span, entries)
    here = jnp.arange(shards * row_count, dtype=jnp.int32) // row_count
    few = shards == 8
    if few:
        first, rest = lax.optimization_barrier((pieces[:, 1], pieces))
        cut = [rest[:, 0], first, rest[:, 2], rest[:, 3]]
        first_hop = [(k, k ^ quarter if k != quarter else k) for k in range(1, shards)]
        arrived = [cut[0]] + [hand(cut[k % quarter], pair) for k, pair in enumerate(first_hop, 1)]
        held = jnp.stack(arrived)
        second_hop = [(0, 0), (1, 1), (2, 2), (3, 3)]
        distance = jnp.array(second_hop, jnp.int32)[:, core % 2]
        order = distance[:, None] ^ (me % quarter)
        order = (order * row_count + jnp.arange(row_count)).reshape(half_rows)
        slots = source ^ me
        slots = jnp.where((core % 2 == 1) & (slots % quarter != 0), slots ^ quarter, slots)
        slots = lax.dynamic_slice_in_dim(
            slots, (me // quarter) * half_rows, half_rows)[order]
        sent = gather_pieces(slots, held, quarter)
        recv = [sent[0]] + [hand(sent[k], second_hop[k]) for k in range(1, quarter)]
        mask = (source ^ here) % quarter
    else:
        pieces = jnp.moveaxis(pieces, 0, 1)
        held = exchange(jnp.concatenate([pieces, pieces]).reshape(
            shards, groups * span, entries)).reshape(shards, groups, span, entries)
        slots = lax.dynamic_slice_in_dim(source, (me // quarter) * half_rows, half_rows)
        sent, = gather_pieces(slots, held, 1)
        sent = exchange(sent.reshape(quarter, row_count * groups * span, entries), halves)
        sent = jnp.moveaxis(sent.reshape(quarter, row_count, groups, span, entries), 0, 2)
        sent = sent.reshape(row_count, groups, 4, quarter * span // 4, entries)
        recv = [sent[:, :, p] for p in range(4)]
        mask = jnp.zeros_like(source)
        distance = jnp.arange(4, dtype=jnp.int32)

    groups = local_heads // (HEADS // GROUPS)
    group_base = lax.axis_index("head") * groups
    ready = prepare(
        x_new, z_gate, dt_raw,
        lax.dynamic_slice_in_dim(b_in, group_base, groups, 2),
        lax.dynamic_slice_in_dim(c_in, group_base, groups, 2),
        a_rate, dt_bias, skip_d)
    info = jnp.concatenate([
        lax.dynamic_slice_in_dim(listed, me * row_count, row_count),
        lax.dynamic_slice_in_dim(mask, me * row_count, row_count), distance])[None]
    resident = resident_states.reshape(row_count, flat, entries)
    gain = norm_gain.reshape(1, flat)
    final, seen = decode((0, 3), info, [recv[0], recv[3]], resident, ready, gain, ())
    decoded, final = decode((1, 2), info, recv[1:3], resident, ready, gain, (seen, final))
    steps = x_new.shape[0]
    decoded = decoded.reshape(steps, row_count, channels, local_heads)
    return (jnp.swapaxes(decoded, 2, 3), final.reshape(resident_states.shape))


def solution(mesh):
    placed = (
        P(("parts", "rows"), "head", None, None),
        P("parts"),
        P("parts"),
        P(("parts", "rows"), "head", None, None),
        P(None, ("parts", "rows"), "head", None),
        P(None, ("parts", "rows"), "head", None),
        P(None, ("parts", "rows"), "head"),
        P(None, ("parts", "rows"), None, None),
        P(None, ("parts", "rows"), None, None),
        P("head"),
        P("head"),
        P("head"),
        P("head", None),
    )
    return jax.shard_map(
        local,
        mesh=mesh,
        in_specs=placed,
        out_specs=(
            P(None, ("parts", "rows"), "head", None),
            P(("parts", "rows"), "head", None, None),
        ),
        check_vma=False,
    )
```
